512 devices in a mesh: gx: 16 (over y, core), gy: 8 (over x, z_hi), view: 4 (over z_lo).
Axes of the slice: x: 4, y: 8, z: 8 (z_hi: 2, z_lo: 4; z = z_hi * 4 + z_lo), core: 2. Of those that a mesh axis runs over, the one named last changes fastest.
Arguments:
- estimate: float32 [512, 512, 128], P('gx', 'gy'), may hold values from 0.5 to 2
- views_data: bfloat16 [4, 512, 512, 128], P('view', 'gx', 'gy'), may hold values from 0.19921875 to 3
- spread_x: float32 [4, 33], P('view'), may hold values from 0.05 to 1
- spread_y: float32 [4, 33], P('view'), may hold values from 0.05 to 1
- spread_z: float32 [4, 33], P('view'), may hold values from 0.05 to 1
Outputs:
- deconvolved: float32 [512, 512, 128], P(('gx', 'view'), 'gy')
The draws below stay inside these ranges and needn't reach their ends.
All inputs are finite; a program needn't handle non-finite values.
Results may differ from the reference program's by a relative error of at most 0.0003.
Values sent between devices are 32-bit elements; how exact they have to be, the bound alone decides.
No kernel may reach another device: no remote copies, remote signals or barrier semaphores. Data moves between devices by JAX's collectives and lax.ppermute only.
A program may use at most 64 MiB of HBM per device.

```python
import math
import jax
import jax.numpy as jnp
from jax import lax

Z = 128
ITERS = 2
TAPS = 33
VIEWS = 4
NX = 512
NY = 512


def levels(stream_key, extent, split, low, largest):
    factor_of = 1.0
    for dim, parts in split:
        draws = jax.random.uniform(jax.random.fold_in(jax.random.fold_in(stream_key, 6), dim), (parts,), jnp.float32, low / len(split), largest / len(split))
        factor_of = factor_of * jnp.repeat(jnp.exp(draws), extent[dim] // parts).reshape((-1,) + (1,) * (len(extent) - 1 - dim))
    return factor_of


def setup_inputs(seed: int = 0) -> dict:
    keys = jax.random.split(jax.random.key(seed), 6)
    return {
        "estimate": jnp.clip(0.5 + 1.5 * jax.random.uniform(keys[0], (NX, NY, Z), jnp.float32) ** levels(keys[0], (NX, NY, Z), ((0, 16), (1, 8)), -0.2, 0.2), 0.5, 2.0),
        "views_data": jnp.clip(0.19921875 + 2.8007812 * jax.random.uniform(keys[1], (VIEWS, NX, NY, Z), jnp.float32) ** levels(keys[1], (VIEWS, NX, NY, Z), ((0, 4), (1, 16), (2, 8)), -0.2, 0.2), 0.19921875, 3.0).astype(jnp.bfloat16),
        "spread_x": jnp.clip(jnp.exp(math.log(1.0) - 2.9957323 * jax.random.uniform(keys[2], (VIEWS, TAPS), jnp.float32) ** levels(keys[2], (VIEWS, TAPS), ((0, 4),), -0.2, 0.2)), 0.05, 1.0),
        "spread_y": jnp.clip(jnp.exp(math.log(1.0) - 2.9957323 * jax.random.uniform(keys[3], (VIEWS, TAPS), jnp.float32) ** levels(keys[3], (VIEWS, TAPS), ((0, 4),), -0.2, 0.2)), 0.05, 1.0),
        "spread_z": jnp.clip(jnp.exp(math.log(1.0) - 2.9957323 * jax.random.uniform(keys[4], (VIEWS, TAPS), jnp.float32) ** levels(keys[4], (VIEWS, TAPS), ((0, 4),), -0.2, 0.2)), 0.05, 1.0),
    }


def blur_axis(volume, weights, axis_number, adjoint):
    half_width = (weights.shape[0] - 1) // 2
    length = volume.shape[axis_number]
    widths = [(0, 0), (0, 0), (0, 0)]
    widths[axis_number] = (half_width, half_width)
    padded = jnp.pad(volume, widths)
    result = jnp.zeros_like(volume)
    for tap_number in range(weights.shape[0]):
        start_row = tap_number if adjoint else 2 * half_width - tap_number
        result = result + weights[tap_number] * lax.slice_in_dim(padded, start_row, start_row + length, axis=axis_number)
    return result


def reference(estimate, views_data, spread_x, spread_y, spread_z):
    kernel_x = spread_x / jnp.sum(spread_x, axis=1, keepdims=True)
    kernel_y = spread_y / jnp.sum(spread_y, axis=1, keepdims=True)
    kernel_z = spread_z / jnp.sum(spread_z, axis=1, keepdims=True)
    for step_number in range(ITERS):
        log_total = jnp.zeros_like(estimate)
        for view_number in range(VIEWS):
            blurred = blur_axis(estimate, kernel_x[view_number], 0, False)
            blurred = blur_axis(blurred, kernel_y[view_number], 1, False)
            blurred = blur_axis(blurred, kernel_z[view_number], 2, False)
            ratios = views_data[view_number].astype(jnp.float32) / blurred
            back_field = blur_axis(ratios, kernel_x[view_number], 0, True)
            back_field = blur_axis(back_field, kernel_y[view_number], 1, True)
            back_field = blur_axis(back_field, kernel_z[view_number], 2, True)
            log_total = log_total + jnp.log(back_field)
        estimate = estimate * jnp.exp(log_total / VIEWS)
    return estimate
```

```python
import functools

import jax
import jax.numpy as jnp
from jax import lax
from jax.experimental import pallas as pl
from jax.experimental.pallas import tpu as pltpu
from jax.sharding import PartitionSpec as P

ITERS = 2
TAPS = 33
HALF = 16
LANES = 128
VMEM = pl.BlockSpec(memory_space=pltpu.VMEM)
SMEM = pl.BlockSpec(memory_space=pltpu.SMEM)


def call(kernel, outs, scratch, *args):
    specs = [SMEM if a.dtype == jnp.int32 else VMEM for a in args]
    return pl.pallas_call(
        kernel,
        out_shape=[jax.ShapeDtypeStruct(s, d) for s, d in outs],
        in_specs=specs,
        out_specs=[VMEM] * len(outs),
        scratch_shapes=scratch,
        compiler_params=pltpu.CompilerParams(vmem_limit_bytes=24 * 2**20),
    )(*args)


def split(value):
    high = value.astype(jnp.bfloat16)
    low = (value - high.astype(jnp.float32)).astype(jnp.bfloat16)
    return high, low


def prepare_kernel(sx_ref, sy_ref, sz_ref, kx_ref, ky_ref, forward_ref, adjoint_ref):
    for source, target in ((sx_ref, kx_ref), (sy_ref, ky_ref)):
        taps = source[...] / jnp.sum(source[...], axis=1, keepdims=True)
        for t in range(TAPS):
            target[t] = jnp.broadcast_to(taps[:, t : t + 1], (8, LANES))
    taps = sz_ref[...] / jnp.sum(sz_ref[...], axis=1, keepdims=True)
    row = lax.broadcasted_iota(jnp.int32, (LANES, LANES), 0)
    column = lax.broadcasted_iota(jnp.int32, (LANES, LANES), 1)
    for target, offset in ((forward_ref, column - row + HALF), (adjoint_ref, row - column + HALF)):
        band = jnp.zeros((LANES, LANES), jnp.float32)
        for t in range(TAPS):
            band = jnp.where(offset == t, jnp.broadcast_to(taps[:, t : t + 1], (LANES, LANES)), band)
        high, low = split(band)
        for k in (0, LANES):
            target[k : k + LANES, :LANES] = high
            target[k : k + LANES, LANES:] = low


def blur_y_row(ext_ref, row, taps_ref, adjoint):
    length = ext_ref.shape[1] - 2 * HALF
    groups = length // 8
    total = None
    for rho in range(8):
        reach = 5 if rho == 0 else 4
        window = ext_ref[row, pl.ds(rho, length + 8 * (reach - 1)), :]
        window = window.reshape(groups + reach - 1, 8, LANES)
        for m in range(reach):
            s = rho + 8 * m
            t = s if adjoint else TAPS - 1 - s
            term = window[m : m + groups] * taps_ref[t]
            total = term if total is None else total + term
    return total.reshape(length, LANES)


def blur_x_block(ext_ref, columns, taps_ref, adjoint, store):
    length = ext_ref.shape[0] - 2 * HALF
    block = 16
    taps = [taps_ref[t] for t in range(TAPS)]
    for first in range(0, length, block):
        totals = [None] * block
        for m in range(block + 2 * HALF):
            value = ext_ref[first + m, columns, :]
            for i in range(block):
                s = m - i
                if 0 <= s < TAPS:
                    t = s if adjoint else TAPS - 1 - s
                    term = value * taps[t]
                    totals[i] = term if totals[i] is None else totals[i] + term
        for i in range(block):
            store(first + i, totals[i])


def blur_z(value, matrix_ref):
    high, low = split(value)
    both = jnp.concatenate([high, low], axis=1)
    product = jnp.dot(both, matrix_ref[...], preferred_element_type=jnp.float32)
    return product[:, :LANES] + product[:, LANES:]


def forward_y_kernel(v_ref, *refs):
    quarters, (before_ref, after_ref, taps_ref, low_ref, high_ref, ext_ref) = refs[:-6], refs[-6:]
    rows, width = before_ref.shape[0], low_ref.shape[1]
    ext_ref[:, :HALF, :] = before_ref[...]
    ext_ref[:, HALF + width :, :] = after_ref[...]
    if len(quarters) == 1:
        ext_ref[:, HALF : HALF + width, :] = quarters[0][...]
    else:
        share = rows // len(quarters)
        for d, quarter in enumerate(quarters):
            place = lax.rem(v_ref[0] + len(quarters) - d, len(quarters)) * share
            ext_ref[pl.ds(place, share), HALF : HALF + width, :] = quarter[...]

    half = rows // 2

    @pl.loop(0, half)
    def _(i):
        low_ref[i] = blur_y_row(ext_ref, i, taps_ref, False)

    @pl.loop(0, half)
    def _(i):
        high_ref[i] = blur_y_row(ext_ref, half + i, taps_ref, False)


def fill_x(ext_ref, before_ref, low_ref, high_ref, after_ref):
    half = low_ref.shape[0]
    ext_ref[:HALF] = before_ref[...]
    ext_ref[HALF : HALF + half] = low_ref[...]
    ext_ref[HALF + half : HALF + 2 * half] = high_ref[...]
    ext_ref[HALF + 2 * half :] = after_ref[...]


def ratio_kernel(before_ref, low_ref, high_ref, after_ref, data_ref, taps_ref, matrix_ref, out_low_ref, out_high_ref, ext_ref, mid_ref):
    fill_x(ext_ref, before_ref, low_ref, high_ref, after_ref)
    rows, width = mid_ref.shape[:2]

    @pl.loop(0, width // 8)
    def _(j):
        columns = pl.ds(pl.multiple_of(j * 8, 8), 8)

        def store(i, value):
            mid_ref[i, columns, :] = value

        blur_x_block(ext_ref, columns, taps_ref, False, store)

    step = 4
    for out_ref, first in ((out_low_ref, 0), (out_high_ref, rows // 2)):

        @pl.loop(0, rows // 2 // step)
        def _(c):
            value = mid_ref[pl.ds(first + c * step, step)].reshape(step * width, LANES)
            blurred = blur_z(value, matrix_ref).reshape(step, width, LANES)
            data = data_ref[pl.ds(first + c * step, step)].astype(jnp.float32)
            out_ref[pl.ds(c * step, step)] = data / blurred


def adjoint_x_kernel(before_ref, low_ref, high_ref, after_ref, taps_ref, out_ref, left_ref, right_ref, ext_ref):
    fill_x(ext_ref, before_ref, low_ref, high_ref, after_ref)
    width = out_ref.shape[1]

    @pl.loop(0, width // 8)
    def _(j):
        columns = pl.ds(pl.multiple_of(j * 8, 8), 8)

        def store(i, value):
            out_ref[i, columns, :] = value

        blur_x_block(ext_ref, columns, taps_ref, True, store)

    left_ref[...] = out_ref[:, :HALF, :]
    right_ref[...] = out_ref[:, width - HALF :, :]


def logs_kernel(v_ref, before_ref, own_ref, after_ref, taps_ref, matrix_ref, *refs):
    outs, (ext_ref, mid_ref) = refs[:-2], refs[-2:]
    rows, width = own_ref.shape[:2]
    ext_ref[:, :HALF, :] = before_ref[...]
    ext_ref[:, HALF : HALF + width, :] = own_ref[...]
    ext_ref[:, HALF + width :, :] = after_ref[...]
    share = rows // len(outs)
    for d, out_ref in enumerate(outs):
        first = lax.rem(v_ref[0] + d, len(outs)) * share

        @pl.loop(0, share)
        def _(i):
            mid_ref[i] = blur_y_row(ext_ref, first + i, taps_ref, True)

        step = 4

        @pl.loop(0, share // step)
        def _(c):
            value = mid_ref[pl.ds(c * step, step)].reshape(step * width, LANES)
            back = blur_z(value, matrix_ref).reshape(step, width, LANES)
            out_ref[pl.ds(c * step, step)] = jnp.log(back)


def shifted(size, by):
    return [(i, i + by) for i in range(size) if 0 <= i + by < size]


def exchange(last, first, axis):
    size = lax.axis_size(axis)
    return lax.ppermute(last, axis, shifted(size, 1)), lax.ppermute(first, axis, shifted(size, -1))


def rotated(value, by):
    size = lax.axis_size("view")
    return lax.ppermute(value, "view", [(i, (i + by) % size) for i in range(size)])


def body(estimate, views_data, spread_x, spread_y, spread_z):
    rows, width, depth = estimate.shape
    views = lax.axis_size("view")
    share = rows // views
    v = lax.axis_index("view")
    v_word = v.astype(jnp.int32).reshape(1)
    data = views_data[0]
    f32 = jnp.float32
    taps_shape = ((TAPS, 8, LANES), f32)
    matrix_shape = ((2 * LANES, 2 * LANES), jnp.bfloat16)
    taps_x, taps_y, forward_z, adjoint_z = call(
        prepare_kernel, [taps_shape, taps_shape, matrix_shape, matrix_shape], [], spread_x, spread_y, spread_z
    )
    half_shape = ((rows // 2, width, depth), f32)
    edge_shape = ((rows, HALF, depth), f32)
    ext_x = pltpu.VMEM((rows + 2 * HALF, width, depth), f32)
    ext_y = pltpu.VMEM((rows, width + 2 * HALF, depth), f32)
    own = lax.dynamic_slice_in_dim(estimate, v * share, share, 0)
    pieces = [estimate]
    edges = (estimate[:, width - HALF :], estimate[:, :HALF])
    for step_number in range(ITERS):
        before, after = exchange(*edges, "gy")
        low, high = call(forward_y_kernel, [half_shape] * 2, [ext_y], v_word, *pieces, before, after, taps_y)
        before, after = exchange(high, low, "gx")
        low, high = call(
            ratio_kernel, [half_shape] * 2, [ext_x, pltpu.VMEM((rows, width, depth), f32)],
            before, low, high, after, data, taps_x, forward_z,
        )
        before, after = exchange(high, low, "gx")
        mid, left, right = call(
            adjoint_x_kernel, [((rows, width, depth), f32), edge_shape, edge_shape], [ext_x],
            before, low, high, after, taps_x,
        )
        before, after = exchange(right, left, "gy")
        terms = call(
            logs_kernel, [((share, width, depth), f32)] * views, [ext_y, pltpu.VMEM((share, width, depth), f32)],
            v_word, before, mid, after, taps_y, adjoint_z,
        )
        total = terms[0]
        for d in range(1, views):
            total = total + rotated(terms[d], d)
        own = own * jnp.exp(total / views)
        if step_number + 1 < ITERS:
            pieces = [own] + [rotated(own, d) for d in range(1, views)]
            whole = jnp.zeros((rows, width, depth), f32)
            for d, piece in enumerate(pieces):
                whole = lax.dynamic_update_slice_in_dim(whole, piece, lax.rem(v + views - d, views) * share, 0)
            edges = (whole[:, width - HALF :], whole[:, :HALF])
    return own


def solution(mesh):
    in_specs = (
        P("gx", "gy", None),
        P("view", "gx", "gy", None),
        P("view", None),
        P("view", None),
        P("view", None),
    )
    out_specs = P(("gx", "view"), "gy", None)
    return jax.shard_map(body, mesh=mesh, in_specs=in_specs, out_specs=out_specs, check_vma=False)
```

```python
import jax
import jax.numpy as jnp
from jax import lax
from jax.experimental import pallas as pl
from jax.experimental.pallas import tpu as pltpu
from jax.sharding import PartitionSpec as P

ITERS = 2
TAPS = 33
HALF = 16
LANES = 128
VMEM = pl.BlockSpec(memory_space=pltpu.VMEM)
SMEM = pl.BlockSpec(memory_space=pltpu.SMEM)


def call(kernel, outs, scratch, *args):
    specs = [SMEM if a.dtype == jnp.int32 else VMEM for a in args]
    return pl.pallas_call(
        kernel,
        out_shape=[jax.ShapeDtypeStruct(s, d) for s, d in outs],
        in_specs=specs,
        out_specs=[VMEM] * len(outs),
        scratch_shapes=scratch,
        compiler_params=pltpu.CompilerParams(vmem_limit_bytes=24 * 2**20),
    )(*args)


def split(value):
    high = value.astype(jnp.bfloat16)
    low = (value - high.astype(jnp.float32)).astype(jnp.bfloat16)
    return high, low


def source(v_ref, d, views):
    return lax.rem(v_ref[0] + views - d, views)


def deal_kernel(v_ref, data_ref, *out_refs):
    views, width = len(out_refs), out_refs[0].shape[1]
    for d, out_ref in enumerate(out_refs):
        first = pl.multiple_of(lax.rem(v_ref[0] + d, views) * width, width)
        out_ref[...] = data_ref[:, pl.ds(first, width), :].astype(jnp.float32)


def prepare_kernel(v_ref, *refs):
    spreads_refs, (taps_x_ref, taps_y_ref, forward_ref, adjoint_ref) = refs[:-4], refs[-4:]
    row = lax.broadcasted_iota(jnp.int32, (LANES, LANES), 0)
    column = lax.broadcasted_iota(jnp.int32, (LANES, LANES), 1)
    for d, spreads_ref in enumerate(spreads_refs):
        view = source(v_ref, d, len(spreads_refs))
        spreads = spreads_ref[:, :TAPS]
        normal = spreads / jnp.sum(spreads, axis=1, keepdims=True)
        for n, target in ((0, taps_x_ref), (1, taps_y_ref)):
            for t in range(TAPS):
                target[view, t] = jnp.broadcast_to(normal[n : n + 1, t : t + 1], (8, LANES))
        for target, offset in ((forward_ref, column - row + HALF), (adjoint_ref, row - column + HALF)):
            band = jnp.zeros((LANES, LANES), jnp.float32)
            for t in range(TAPS):
                tap = jnp.broadcast_to(normal[2:3, t : t + 1], (LANES, LANES))
                band = jnp.where(offset == t, tap, band)
            high, low = split(band)
            for k in (0, LANES):
                target[view, k : k + LANES, :LANES] = high
                target[view, k : k + LANES, LANES:] = low


def blur_y(ext_ref, rows, taps, adjoint):
    width = ext_ref.shape[1] - 2 * HALF
    groups = width // 8
    totals = [None] * len(taps)
    for rho in range(8):
        reach = 5 if rho == 0 else 4
        window = ext_ref[rows, pl.ds(rho, width + 8 * (reach - 1)), :]
        window = window.reshape(window.shape[0], groups + reach - 1, 8, LANES)
        for m in range(reach):
            s = rho + 8 * m
            t = s if adjoint else TAPS - 1 - s
            for n, tap in enumerate(taps):
                term = window[:, m : m + groups] * tap(t)
                totals[n] = term if totals[n] is None else totals[n] + term
    return [total.reshape(total.shape[0], width, LANES) for total in totals]


def blur_x(load, tap, adjoint, length, store):
    block = 16
    taps = [tap(t) for t in range(TAPS)]
    for first in range(0, length, block):
        totals = [None] * block
        for m in range(block + 2 * HALF):
            value = load(first + m)
            for i in range(block):
                s = m - i
                if 0 <= s < TAPS:
                    term = value * taps[s if adjoint else TAPS - 1 - s]
                    totals[i] = term if totals[i] is None else totals[i] + term
        for i in range(block):
            store(first + i, totals[i])


def blur_z(value, matrix):
    rows, width, _ = value.shape
    high, low = split(value.reshape(rows * width, LANES))
    product = jnp.dot(jnp.concatenate([high, low], axis=1), matrix, preferred_element_type=jnp.float32)
    return (product[:, :LANES] + product[:, LANES:]).reshape(rows, width, LANES)


def forward_y_kernel(before_ref, own_ref, after_ref, taps_ref, low_ref, high_ref, ext_ref):
    rows, width = own_ref.shape[:2]
    views, half = low_ref.shape[:2]
    ext_ref[:, :HALF, :] = before_ref[...]
    ext_ref[:, HALF : HALF + width, :] = own_ref[...]
    ext_ref[:, HALF + width :, :] = after_ref[...]
    taps = [lambda t, view=view: taps_ref[view, t] for view in range(views)]
    block = 2
    for out_ref, first in ((low_ref, 0), (high_ref, half)):

        @pl.loop(0, half // block)
        def _(i):
            for view, blurred in enumerate(blur_y(ext_ref, pl.ds(first + i * block, block), taps, False)):
                out_ref[view, pl.ds(i * block, block)] = blurred


def loop_x(refs, taps_ref, adjoint, out_ref):
    views, rows, width, _ = out_ref.shape
    groups = width // 8

    @pl.loop(0, views * groups)
    def _(n):
        view = n // groups
        columns = pl.ds(pl.multiple_of(lax.rem(n, groups) * 8, 8), 8)

        def load(m):
            return refs[m // HALF][view, m % HALF, columns, :]

        def store(i, value):
            out_ref[view, i, columns, :] = value

        blur_x(load, lambda t: taps_ref[view, t], adjoint, rows, store)


def ratio_kernel(v_ref, before_ref, low_ref, high_ref, after_ref, taps_ref, matrix_ref, *refs):
    data_refs, (out_low_ref, out_high_ref, mid_ref) = refs[:-3], refs[-3:]
    loop_x((before_ref, low_ref, high_ref, after_ref), taps_ref, False, mid_ref)
    half = out_low_ref.shape[1]
    for d, data_ref in enumerate(data_refs):
        view = source(v_ref, d, len(data_refs))
        for out_ref, first in ((out_low_ref, 0), (out_high_ref, half)):
            blurred = blur_z(mid_ref[view, pl.ds(first, half)], matrix_ref[view])
            out_ref[view] = data_ref[pl.ds(first, half)] / blurred


def adjoint_x_kernel(before_ref, low_ref, high_ref, after_ref, taps_ref, out_ref):
    loop_x((before_ref, low_ref, high_ref, after_ref), taps_ref, True, out_ref)


def update_kernel(v_ref, before_ref, own_ref, after_ref, taps_ref, matrix_ref, estimate_ref, *refs):
    outs, (ext_ref, mid_ref, total_ref) = refs[:-3], refs[-3:]
    views, rows, width, _ = own_ref.shape
    block = 4

    @pl.loop(0, views)
    def _(view):
        ext_ref[:, :HALF, :] = before_ref[view]
        ext_ref[:, HALF : HALF + width, :] = own_ref[view]
        ext_ref[:, HALF + width :, :] = after_ref[view]

        @pl.loop(0, rows // block)
        def _(i):
            there = pl.ds(i * block, block)
            mid_ref[there] = blur_y(ext_ref, there, [lambda t: taps_ref[view, t]], True)[0]

        for first in range(0, rows, HALF):
            there = pl.ds(first, HALF)
            terms = jnp.log(blur_z(mid_ref[there], matrix_ref[view]))
            total_ref[there] = jnp.where(view == 0, terms, terms + total_ref[there])

    share = rows // len(outs)
    for d, out_ref in enumerate(outs):
        there = pl.ds(lax.rem(v_ref[0] + d, len(outs)) * share, share)
        out_ref[...] = estimate_ref[there] * jnp.exp(total_ref[there] / views)


def collect_kernel(v_ref, *refs):
    pieces, out_ref = refs[:-1], refs[-1]
    width = pieces[0].shape[1]
    for d, piece in enumerate(pieces):
        first = pl.multiple_of(source(v_ref, d, len(pieces)) * width, width)
        out_ref[:, pl.ds(first, width), :] = piece[...]


def shifted(size, by):
    return [(i, i + by) for i in range(size) if 0 <= i + by < size]


def exchange(last, first, axes):
    size = lax.axis_size(axes)
    return lax.ppermute(last, axes, shifted(size, 1)), lax.ppermute(first, axes, shifted(size, -1))


def rotated(pieces):
    size = len(pieces)
    return [pieces[0]] + [
        lax.ppermute(pieces[d], "view", [(i, (i + d) % size) for i in range(size)]) for d in range(1, size)
    ]


def body(estimate, views_data, spread_x, spread_y, spread_z):
    rows, width, depth = estimate.shape
    views = lax.axis_size("view")
    width = width // views
    assert width == HALF and rows == 2 * HALF and depth == LANES
    f32 = jnp.float32
    v = lax.axis_index("view")
    v_word = v.astype(jnp.int32).reshape(1)
    part_shape = ((rows, width, depth), f32)
    all_shape = ((views, rows, width, depth), f32)
    half_shape = ((views, rows // 2, width, depth), f32)
    taps_shape = ((views, TAPS, 8, LANES), f32)
    matrix_shape = ((views, 2 * LANES, 2 * LANES), jnp.bfloat16)
    ext = pltpu.VMEM((rows, width + 2 * HALF, depth), f32)

    own = lax.dynamic_slice_in_dim(estimate, v * width, width, 1)
    spreads = jnp.concatenate([spread_x, spread_y, spread_z, jnp.ones((5, TAPS), f32)])
    spreads = rotated([jnp.pad(spreads, ((0, 0), (0, LANES - TAPS)))] * views)
    data = rotated(call(deal_kernel, [part_shape] * views, [], v_word, views_data[0]))
    taps_x, taps_y, forward_z, adjoint_z = call(
        prepare_kernel, [taps_shape, taps_shape, matrix_shape, matrix_shape], [], v_word, *spreads
    )
    for step_number in range(ITERS):
        before, after = exchange(own, own, ("gy", "view"))
        low, high = call(forward_y_kernel, [half_shape] * 2, [ext], before, own, after, taps_y)
        before, after = exchange(high, low, "gx")
        low, high = call(
            ratio_kernel, [half_shape] * 2, [pltpu.VMEM(*all_shape)],
            v_word, before, low, high, after, taps_x, forward_z, *data,
        )
        before, after = exchange(high, low, "gx")
        mid = call(adjoint_x_kernel, [all_shape], [], before, low, high, after, taps_x)[0]
        before, after = exchange(mid, mid, ("gy", "view"))
        last_step = step_number + 1 == ITERS
        pieces = [((rows // views, width, depth), f32)] * views if last_step else [part_shape]
        own, *others = call(
            update_kernel, pieces, [ext, pltpu.VMEM(*part_shape), pltpu.VMEM(*part_shape)],
            v_word, before, mid, after, taps_y, adjoint_z, own,
        )
    pieces = rotated([own, *others])
    return call(collect_kernel, [((rows // views, width * views, depth), f32)], [], v_word, *pieces)[0]


def solution(mesh):
    in_specs = (
        P("gx", "gy", None),
        P("view", "gx", "gy", None),
        P("view", None),
        P("view", None),
        P("view", None),
    )
    out_specs = P(("gx", "view"), "gy", None)
    return jax.shard_map(body, mesh=mesh, in_specs=in_specs, out_specs=out_specs, check_vma=False)
```

```python
import functools

import jax
import jax.numpy as jnp
from jax import lax
from jax.experimental import pallas as pl
from jax.experimental.pallas import tpu as pltpu
from jax.sharding import PartitionSpec as P

ITERS = 2
TAPS = 33
HALF = 16
LANES = 128
VMEM = pl.BlockSpec(memory_space=pltpu.VMEM)
SMEM = pl.BlockSpec(memory_space=pltpu.SMEM)


def call(kernel, outs, scratch, *args):
    specs = [SMEM if a.dtype == jnp.int32 else VMEM for a in args]
    return pl.pallas_call(
        kernel,
        out_shape=[jax.ShapeDtypeStruct(s, d) for s, d in outs],
        in_specs=specs,
        out_specs=[VMEM] * len(outs),
        scratch_shapes=scratch,
        compiler_params=pltpu.CompilerParams(vmem_limit_bytes=24 * 2**20),
    )(*args)


def split(value):
    high = value.astype(jnp.bfloat16)
    low = (value - high.astype(jnp.float32)).astype(jnp.bfloat16)
    return high, low


def deal_kernel(data_ref, out_ref):
    views, _, width, _ = out_ref.shape
    for view in range(views):
        out_ref[view] = data_ref[:, view * width : (view + 1) * width, :].astype(jnp.float32)


def prepare_kernel(spreads_ref, taps_x_ref, taps_y_ref, forward_ref, adjoint_ref):
    row = lax.broadcasted_iota(jnp.int32, (LANES, LANES), 0)
    column = lax.broadcasted_iota(jnp.int32, (LANES, LANES), 1)
    for view in range(spreads_ref.shape[0]):
        spreads = spreads_ref[view, :, :TAPS]
        normal = spreads / jnp.sum(spreads, axis=1, keepdims=True)
        for n, target in ((0, taps_x_ref), (1, taps_y_ref)):
            for t in range(TAPS):
                target[view, t] = jnp.broadcast_to(normal[n : n + 1, t : t + 1], (8, LANES))
        for target, offset in ((forward_ref, column - row + HALF), (adjoint_ref, row - column + HALF)):
            band = jnp.zeros((LANES, LANES), jnp.float32)
            for t in range(TAPS):
                tap = jnp.broadcast_to(normal[2:3, t : t + 1], (LANES, LANES))
                band = jnp.where(offset == t, tap, band)
            high, low = split(band)
            for k in (0, LANES):
                target[view, k : k + LANES, :LANES] = high
                target[view, k : k + LANES, LANES:] = low


def blur_y(ext_ref, rows, taps, adjoint):
    width = ext_ref.shape[1] - 2 * HALF
    groups = width // 8
    totals = [None] * len(taps)
    for rho in range(8):
        reach = 5 if rho == 0 else 4
        window = ext_ref[rows, pl.ds(rho, width + 8 * (reach - 1)), :]
        window = window.reshape(window.shape[0], groups + reach - 1, 8, LANES)
        for m in range(reach):
            s = rho + 8 * m
            t = s if adjoint else TAPS - 1 - s
            for n, tap in enumerate(taps):
                term = window[:, m : m + groups] * tap(t)
                totals[n] = term if totals[n] is None else totals[n] + term
    return [total.reshape(total.shape[0], width, LANES) for total in totals]


def blur_x(load, tap, adjoint, length, store):
    block = 16
    taps = [tap(t) for t in range(TAPS)]
    for first in range(0, length, block):
        totals = [None] * block
        for m in range(block + 2 * HALF):
            value = load(first + m)
            for i in range(block):
                s = m - i
                if 0 <= s < TAPS:
                    term = value * taps[s if adjoint else TAPS - 1 - s]
                    totals[i] = term if totals[i] is None else totals[i] + term
        for i in range(block):
            store(first + i, totals[i])


def blur_z(value, matrix):
    rows, width, _ = value.shape
    high, low = split(value.reshape(rows * width, LANES))
    product = jnp.dot(jnp.concatenate([high, low], axis=1), matrix, preferred_element_type=jnp.float32)
    return (product[:, :LANES] + product[:, LANES:]).reshape(rows, width, LANES)


def forward_y(ext_ref, taps_ref, out_ref):
    views, rows = out_ref.shape[:2]
    taps = [lambda t, view=view: taps_ref[view, t] for view in range(views)]
    block = 2

    @pl.loop(0, rows // block)
    def _(i):
        there = pl.ds(i * block, block)
        for view, blurred in enumerate(blur_y(ext_ref, there, taps, False)):
            out_ref[view, there] = blurred


def forward_y_kernel(before_ref, own_ref, after_ref, taps_ref, out_ref, ext_ref):
    width = own_ref.shape[1]
    ext_ref[:, :HALF, :] = before_ref[...]
    ext_ref[:, HALF : HALF + width, :] = own_ref[...]
    ext_ref[:, HALF + width :, :] = after_ref[...]
    forward_y(ext_ref, taps_ref, out_ref)


def first_forward_y_kernel(first, v_ref, tile_ref, across_ref, taps_ref, out_ref, ext_ref):
    rows, width = out_ref.shape[1:3]
    views = tile_ref.shape[1] // width
    there = pl.ds(first, rows)
    for n in range(3):
        place = v_ref[0] + n - 1
        inside = jnp.logical_and(place >= 0, place < views)

        @pl.when(inside)
        def _():
            columns = pl.ds(pl.multiple_of(place * width, width), width)
            ext_ref[:, n * width : (n + 1) * width, :] = tile_ref[there, columns, :]

        @pl.when(jnp.logical_not(inside))
        def _():
            ext_ref[:, n * width : (n + 1) * width, :] = across_ref[there]

    forward_y(ext_ref, taps_ref, out_ref)


def loop_x(refs, taps_ref, adjoint, out_ref):
    views, rows, width, _ = out_ref.shape
    groups = width // 8

    @pl.loop(0, views * groups)
    def _(n):
        view = n // groups
        columns = pl.ds(pl.multiple_of(lax.rem(n, groups) * 8, 8), 8)

        def load(m):
            return refs[m // HALF][view, m % HALF, columns, :]

        def store(i, value):
            out_ref[view, i, columns, :] = value

        blur_x(load, lambda t: taps_ref[view, t], adjoint, rows, store)


def ratio_kernel(first, before_ref, own_ref, after_ref, taps_ref, matrix_ref, data_ref, out_ref, mid_ref):
    loop_x((before_ref, own_ref, after_ref), taps_ref, False, mid_ref)
    views, rows = out_ref.shape[:2]
    for view in range(views):
        out_ref[view] = data_ref[view, pl.ds(first, rows)] / blur_z(mid_ref[view], matrix_ref[view])


def adjoint_x_kernel(before_ref, own_ref, after_ref, taps_ref, out_ref):
    loop_x((before_ref, own_ref, after_ref), taps_ref, True, out_ref)


def corrected(before_ref, own_ref, after_ref, taps_ref, matrix_ref, estimate_ref, ext_ref, mid_ref, total_ref):
    views, rows, width, _ = own_ref.shape
    block = 4

    @pl.loop(0, views)
    def _(view):
        ext_ref[:, :HALF, :] = before_ref[view]
        ext_ref[:, HALF : HALF + width, :] = own_ref[view]
        ext_ref[:, HALF + width :, :] = after_ref[view]

        @pl.loop(0, rows // block)
        def _(i):
            there = pl.ds(i * block, block)
            mid_ref[there] = blur_y(ext_ref, there, [lambda t: taps_ref[view, t]], True)[0]

        terms = jnp.log(blur_z(mid_ref[...], matrix_ref[view]))
        total_ref[...] = jnp.where(view == 0, terms, terms + total_ref[...])

    return estimate_ref[...] * jnp.exp(total_ref[...] / views)


def update_kernel(before_ref, own_ref, after_ref, taps_ref, matrix_ref, estimate_ref, out_ref, *scratch):
    out_ref[...] = corrected(before_ref, own_ref, after_ref, taps_ref, matrix_ref, estimate_ref, *scratch)


def collect_kernel(pieces_ref, out_ref):
    views, _, width, _ = pieces_ref.shape
    for view in range(views):
        out_ref[:, view * width : (view + 1) * width, :] = pieces_ref[view]


def shifted(size, by):
    return [(i, i + by) for i in range(size) if 0 <= i + by < size]


def onward(value, axes):
    return lax.ppermute(value, axes, shifted(lax.axis_size(axes), 1))


def back(value, axes):
    return lax.ppermute(value, axes, shifted(lax.axis_size(axes), -1))


def across(value):
    tiles, views = lax.axis_size("gy"), lax.axis_size("view")
    pairs = [(gy * views + views - 1, (gy + 1) * views) for gy in range(tiles - 1)]
    return lax.ppermute(value, ("gy", "view"), pairs + [(b, a) for a, b in pairs])


def exchanged(pieces):
    return lax.all_to_all(pieces, "view", 0, 0, tiled=True)


def body(estimate, views_data, spread_x, spread_y, spread_z):
    rows, width, depth = estimate.shape
    views = lax.axis_size("view")
    width = width // views
    half = rows // 2
    assert width == HALF and half == HALF and depth == LANES
    f32 = jnp.float32
    v = lax.axis_index("view")
    v_word = v.astype(jnp.int32).reshape(1)
    y = ("gy", "view")
    half_shape = ((views, half, width, depth), f32)
    taps_shape = ((views, TAPS, 8, LANES), f32)
    matrix_shape = ((views, 2 * LANES, 2 * LANES), jnp.bfloat16)
    part = ((half, width, depth), f32)
    ext = pltpu.VMEM((half, width + 2 * HALF, depth), f32)

    own = lax.dynamic_slice_in_dim(estimate, v * width, width, 1)
    spreads = jnp.concatenate([spread_x, spread_y, spread_z, jnp.ones((5, TAPS), f32)])
    spreads = exchanged(jnp.broadcast_to(jnp.pad(spreads, ((0, 0), (0, LANES - TAPS))), (views, 8, LANES)))
    beside = across(own)
    data = exchanged(call(deal_kernel, [((views, rows, width, depth), f32)], [], views_data[0])[0])
    taps_x, taps_y, forward_z, adjoint_z = call(
        prepare_kernel, [taps_shape, taps_shape, matrix_shape, matrix_shape], [], spreads
    )
    own = [own[:half], own[half:]]
    for step_number in range(ITERS):
        if step_number == 0:
            blurred = [
                call(functools.partial(first_forward_y_kernel, n * half), [half_shape], [ext], v_word, estimate, beside, taps_y)[0]
                for n in range(2)
            ]
        else:
            edges = [(onward(own[n], y), back(own[n], y)) for n in range(2)]
            blurred = [
                call(forward_y_kernel, [half_shape], [ext], edges[n][0], own[n], edges[n][1], taps_y)[0] for n in range(2)
            ]
        low, high = blurred
        before, after = onward(high, "gx"), back(low, "gx")
        mid = [pltpu.VMEM(*half_shape)]
        ratio_low = call(
            functools.partial(ratio_kernel, 0), [half_shape], mid, before, low, high, taps_x, forward_z, data
        )[0]
        ratio_high = call(
            functools.partial(ratio_kernel, half), [half_shape], mid, low, high, after, taps_x, forward_z, data
        )[0]
        before, after = onward(ratio_high, "gx"), back(ratio_low, "gx")
        high = call(adjoint_x_kernel, [half_shape], [], ratio_low, ratio_high, after, taps_x)[0]
        low = call(adjoint_x_kernel, [half_shape], [], before, ratio_low, ratio_high, taps_x)[0]
        ins = [(onward(value, y), value, back(value, y), taps_y, adjoint_z) for value in (low, high)]
        scratch = [ext, pltpu.VMEM(*part), pltpu.VMEM(*part)]
        own = [call(update_kernel, [part], scratch, *ins[n], own[n])[0] for n in range(2)]
    share = rows // views
    pieces = exchanged(jnp.concatenate(own).reshape(views, share, width, depth))
    return call(collect_kernel, [((share, width * views, depth), f32)], [], pieces)[0]


def solution(mesh):
    in_specs = (
        P("gx", "gy", None),
        P("view", "gx", "gy", None),
        P("view", None),
        P("view", None),
        P("view", None),
    )
    out_specs = P(("gx", "view"), "gy", None)
    return jax.shard_map(body, mesh=mesh, in_specs=in_specs, out_specs=out_specs, check_vma=False)
```

```python
import functools

import jax
import jax.numpy as jnp
from jax import lax
from jax.experimental import pallas as pl
from jax.experimental.pallas import tpu as pltpu
from jax.sharding import PartitionSpec as P

ITERS = 2
TAPS = 33
HALF = 16
LANES = 128
VMEM = pl.BlockSpec(memory_space=pltpu.VMEM)
SMEM = pl.BlockSpec(memory_space=pltpu.SMEM)


def call(kernel, outs, scratch, *args):
    specs = [SMEM if a.dtype == jnp.int32 else VMEM for a in args]
    return pl.pallas_call(
        kernel,
        out_shape=[jax.ShapeDtypeStruct(s, d) for s, d in outs],
        in_specs=specs,
        out_specs=[VMEM] * len(outs),
        scratch_shapes=scratch,
        compiler_params=pltpu.CompilerParams(vmem_limit_bytes=10 * 2**20),
    )(*args)


def split(value):
    high = value.astype(jnp.bfloat16)
    low = (value - high.astype(jnp.float32)).astype(jnp.bfloat16)
    return high, low


def deal_kernel(data_ref, out_ref):
    views, _, width, _ = out_ref.shape
    for view in range(views):
        out_ref[view] = data_ref[:, view * width : (view + 1) * width, :].astype(jnp.float32)


def part_kernel(v_ref, tile_ref, out_ref):
    width = out_ref.shape[1]
    out_ref[...] = tile_ref[:, pl.ds(pl.multiple_of(v_ref[0] * width, width), width), :]


def normal_taps(spreads_ref, view):
    spreads = spreads_ref[view, :, :TAPS]
    return spreads / jnp.sum(spreads, axis=1, keepdims=True)


def taps_kernel(spreads_ref, taps_x_ref, taps_y_ref):
    for view in range(spreads_ref.shape[0]):
        normal = normal_taps(spreads_ref, view)
        for n, target in ((0, taps_x_ref), (1, taps_y_ref)):
            for t in range(TAPS):
                target[view, t] = jnp.broadcast_to(normal[n : n + 1, t : t + 1], (8, LANES))


def matrices_kernel(spreads_ref, forward_ref, adjoint_ref):
    row = lax.broadcasted_iota(jnp.int32, (LANES, LANES), 0)
    column = lax.broadcasted_iota(jnp.int32, (LANES, LANES), 1)
    for view in range(spreads_ref.shape[0]):
        normal = normal_taps(spreads_ref, view)
        for target, offset in ((forward_ref, column - row + HALF), (adjoint_ref, row - column + HALF)):
            band = jnp.zeros((LANES, LANES), jnp.float32)
            for t in range(TAPS):
                tap = jnp.broadcast_to(normal[2:3, t : t + 1], (LANES, LANES))
                band = jnp.where(offset == t, tap, band)
            high, low = split(band)
            for k in (0, LANES):
                target[view, k : k + LANES, :LANES] = high
                target[view, k : k + LANES, LANES:] = low


def blur_y(ext_ref, rows, taps, adjoint):
    width = ext_ref.shape[1] - 2 * HALF
    groups = width // 8
    totals = [None] * len(taps)
    for rho in range(8):
        reach = 5 if rho == 0 else 4
        window = ext_ref[rows, pl.ds(rho, width + 8 * (reach - 1)), :]
        window = window.reshape(window.shape[0], groups + reach - 1, 8, LANES)
        for m in range(reach):
            s = rho + 8 * m
            t = s if adjoint else TAPS - 1 - s
            for n, tap in enumerate(taps):
                term = window[:, m : m + groups] * tap(t)
                totals[n] = term if totals[n] is None else totals[n] + term
    return [total.reshape(total.shape[0], width, LANES) for total in totals]


def blur_x(load, tap, adjoint, length, store):
    block = 16
    taps = [tap(t) for t in range(TAPS)]
    for first in range(0, length, block):
        totals = [None] * block
        for m in range(block + 2 * HALF):
            value = load(first + m)
            for i in range(block):
                s = m - i
                if 0 <= s < TAPS:
                    term = value * taps[s if adjoint else TAPS - 1 - s]
                    totals[i] = term if totals[i] is None else totals[i] + term
        for i in range(block):
            store(first + i, totals[i])


def blur_z(value, matrix):
    rows, width, _ = value.shape
    high, low = split(value.reshape(rows * width, LANES))
    product = jnp.dot(jnp.concatenate([high, low], axis=1), matrix, preferred_element_type=jnp.float32)
    return (product[:, :LANES] + product[:, LANES:]).reshape(rows, width, LANES)


def forward_y(ext_ref, taps_ref, out_ref):
    views, rows = out_ref.shape[:2]
    taps = [lambda t, view=view: taps_ref[view, t] for view in range(views)]
    block = 2

    @pl.loop(0, rows // block)
    def _(i):
        there = pl.ds(i * block, block)
        for view, blurred in enumerate(blur_y(ext_ref, there, taps, False)):
            out_ref[view, there] = blurred


def forward_y_kernel(before_ref, own_ref, after_ref, taps_ref, out_ref, ext_ref):
    width = own_ref.shape[1]
    ext_ref[:, :HALF, :] = before_ref[...]
    ext_ref[:, HALF : HALF + width, :] = own_ref[...]
    ext_ref[:, HALF + width :, :] = after_ref[...]
    forward_y(ext_ref, taps_ref, out_ref)


def first_forward_y_kernel(first, v_ref, tile_ref, across_ref, taps_ref, out_ref, ext_ref):
    rows, width = out_ref.shape[1:3]
    views = tile_ref.shape[1] // width
    there = pl.ds(first, rows)
    for n in range(3):
        place = v_ref[0] + n - 1
        inside = jnp.logical_and(place >= 0, place < views)

        @pl.when(inside)
        def _():
            columns = pl.ds(pl.multiple_of(place * width, width), width)
            ext_ref[:, n * width : (n + 1) * width, :] = tile_ref[there, columns, :]

        @pl.when(jnp.logical_not(inside))
        def _():
            ext_ref[:, n * width : (n + 1) * width, :] = across_ref[there]

    forward_y(ext_ref, taps_ref, out_ref)


def loop_x(refs, taps_ref, adjoint, out_ref):
    views, rows, width, _ = out_ref.shape
    groups = width // 8

    @pl.loop(0, views * groups)
    def _(n):
        view = n // groups
        columns = pl.ds(pl.multiple_of(lax.rem(n, groups) * 8, 8), 8)

        def load(m):
            return refs[m // HALF][view, m % HALF, columns, :]

        def store(i, value):
            out_ref[view, i, columns, :] = value

        blur_x(load, lambda t: taps_ref[view, t], adjoint, rows, store)


def ratio_kernel(first, before_ref, own_ref, after_ref, taps_ref, matrix_ref, data_ref, out_ref, mid_ref):
    loop_x((before_ref, own_ref, after_ref), taps_ref, False, mid_ref)
    views, rows = out_ref.shape[:2]
    for view in range(views):
        out_ref[view] = data_ref[view, pl.ds(first, rows)] / blur_z(mid_ref[view], matrix_ref[view])


def blurred_kernel(before_ref, own_ref, after_ref, taps_ref, matrix_ref, out_ref, mid_ref):
    loop_x((before_ref, own_ref, after_ref), taps_ref, False, mid_ref)
    for view in range(out_ref.shape[0]):
        out_ref[view] = blur_z(mid_ref[view], matrix_ref[view])


def divide_kernel(first, data_ref, blurred_ref, out_ref):
    views, rows = out_ref.shape[:2]
    for view in range(views):
        out_ref[view] = data_ref[view, pl.ds(first, rows)] / blurred_ref[view]


def adjoint_x_kernel(before_ref, own_ref, after_ref, taps_ref, out_ref):
    loop_x((before_ref, own_ref, after_ref), taps_ref, True, out_ref)


def update_kernel(
    first, before_ref, own_ref, after_ref, taps_ref, matrix_ref, estimate_ref, out_ref, ext_ref, mid_ref, total_ref
):
    views, rows, width, _ = own_ref.shape
    block = 4

    @pl.loop(0, views)
    def _(view):
        ext_ref[:, :HALF, :] = before_ref[view]
        ext_ref[:, HALF : HALF + width, :] = own_ref[view]
        ext_ref[:, HALF + width :, :] = after_ref[view]

        @pl.loop(0, rows // block)
        def _(i):
            there = pl.ds(i * block, block)
            mid_ref[there] = blur_y(ext_ref, there, [lambda t: taps_ref[view, t]], True)[0]

        terms = jnp.log(blur_z(mid_ref[...], matrix_ref[view]))
        total_ref[...] = jnp.where(view == 0, terms, terms + total_ref[...])

    out_ref[...] = estimate_ref[pl.ds(first, rows)] * jnp.exp(total_ref[...] / views)


def collect_kernel(pieces_ref, out_ref):
    views, _, width, _ = pieces_ref.shape
    for view in range(views):
        out_ref[:, view * width : (view + 1) * width, :] = pieces_ref[view]


def shifted(size, by):
    return [(i, i + by) for i in range(size) if 0 <= i + by < size]


def onward(value, axes):
    return lax.ppermute(value, axes, shifted(lax.axis_size(axes), 1))


def back(value, axes):
    return lax.ppermute(value, axes, shifted(lax.axis_size(axes), -1))


def across(value):
    tiles, views = lax.axis_size("gy"), lax.axis_size("view")
    pairs = [(gy * views + views - 1, (gy + 1) * views) for gy in range(tiles - 1)]
    return lax.ppermute(value, ("gy", "view"), pairs + [(b, a) for a, b in pairs])


def exchanged(pieces):
    return lax.all_to_all(pieces, "view", 0, 0, tiled=True)


def body(estimate, views_data, spread_x, spread_y, spread_z):
    rows, width, depth = estimate.shape
    views = lax.axis_size("view")
    width = width // views
    half = rows // 2
    assert width == HALF and half == HALF and depth == LANES
    f32 = jnp.float32
    v = lax.axis_index("view")
    v_word = v.astype(jnp.int32).reshape(1)
    y = ("gy", "view")
    half_shape = ((views, half, width, depth), f32)
    taps_shape = ((views, TAPS, 8, LANES), f32)
    matrix_shape = ((views, 2 * LANES, 2 * LANES), jnp.bfloat16)
    part = ((half, width, depth), f32)
    ext = pltpu.VMEM((half, width + 2 * HALF, depth), f32)

    own = call(part_kernel, [((rows, width, depth), f32)], [], v_word, estimate)[0]
    spreads = jnp.concatenate([spread_x, spread_y, spread_z, jnp.ones((5, TAPS), f32)])
    spreads = jnp.broadcast_to(jnp.pad(spreads, ((0, 0), (0, LANES - TAPS))), (views, 8, LANES))
    data = call(deal_kernel, [((views, rows, width, depth), f32)], [], views_data[0])[0]
    spreads = exchanged(spreads)
    data = exchanged(data)
    beside = across(own)
    taps_x, taps_y = call(taps_kernel, [taps_shape, taps_shape], [], spreads)
    forward_z, adjoint_z = call(matrices_kernel, [matrix_shape, matrix_shape], [], spreads)
    for step_number in range(ITERS):
        if step_number == 0:
            blurred = [
                call(functools.partial(first_forward_y_kernel, n * half), [half_shape], [ext], v_word, estimate, beside, taps_y)[0]
                for n in range(2)
            ]
        else:
            edges = [(onward(own[n], y), back(own[n], y)) for n in range(2)]
            blurred = [
                call(forward_y_kernel, [half_shape], [ext], edges[n][0], own[n], edges[n][1], taps_y)[0] for n in range(2)
            ]
        low, high = blurred
        before, after = onward(high, "gx"), back(low, "gx")
        mid = [pltpu.VMEM(*half_shape)]
        ratios = []
        for first, rows_in in ((0, (before, low, high)), (half, (low, high, after))):
            if step_number == 0:
                blurred = call(blurred_kernel, [half_shape], mid, *rows_in, taps_x, forward_z)[0]
                ratios.append(call(functools.partial(divide_kernel, first), [half_shape], [], data, blurred)[0])
            else:
                kernel = functools.partial(ratio_kernel, first)
                ratios.append(call(kernel, [half_shape], mid, *rows_in, taps_x, forward_z, data)[0])
        ratio_low, ratio_high = ratios
        before, after = onward(ratio_high, "gx"), back(ratio_low, "gx")
        high = call(adjoint_x_kernel, [half_shape], [], ratio_low, ratio_high, after, taps_x)[0]
        low = call(adjoint_x_kernel, [half_shape], [], before, ratio_low, ratio_high, taps_x)[0]
        ins = [(onward(value, y), value, back(value, y), taps_y, adjoint_z) for value in (low, high)]
        scratch = [ext, pltpu.VMEM(*part), pltpu.VMEM(*part)]
        olds = [(0, own[0]), (0, own[1])] if step_number else [(0, own), (half, own)]
        own = [
            call(functools.partial(update_kernel, first), [part], scratch, *ins[n], old)[0]
            for n, (first, old) in enumerate(olds)
        ]
    share = rows // views
    pieces = exchanged(jnp.concatenate(own).reshape(views, share, width, depth))
    return call(collect_kernel, [((share, width * views, depth), f32)], [], pieces)[0]


def solution(mesh):
    in_specs = (
        P("gx", "gy", None),
        P("view", "gx", "gy", None),
        P("view", None),
        P("view", None),
        P("view", None),
    )
    out_specs = P(("gx", "view"), "gy", None)
    return jax.shard_map(body, mesh=mesh, in_specs=in_specs, out_specs=out_specs, check_vma=False)
```

```python
import functools

import jax
import jax.numpy as jnp
from jax import lax
from jax.experimental import pallas as pl
from jax.experimental.pallas import tpu as pltpu
from jax.sharding import PartitionSpec as P

ITERS = 2
TAPS = 33
HALF = 16
LANES = 128
VMEM = pl.BlockSpec(memory_space=pltpu.VMEM)
SMEM = pl.BlockSpec(memory_space=pltpu.SMEM)


def call(kernel, outs, scratch, *args):
    specs = [SMEM if a.dtype == jnp.int32 else VMEM for a in args]
    return pl.pallas_call(
        kernel,
        out_shape=[jax.ShapeDtypeStruct(s, d) for s, d in outs],
        in_specs=specs,
        out_specs=[VMEM] * len(outs),
        scratch_shapes=scratch,
        compiler_params=pltpu.CompilerParams(vmem_limit_bytes=10 * 2**20),
    )(*args)


def split(value):
    high = value.astype(jnp.bfloat16)
    low = (value - high.astype(jnp.float32)).astype(jnp.bfloat16)
    return high, low


def deal_kernel(data_ref, out_ref):
    views, _, width, _ = out_ref.shape
    for view in range(views):
        out_ref[view] = data_ref[:, view * width : (view + 1) * width, :].astype(jnp.float32)


def part_kernel(v_ref, tile_ref, out_ref):
    width = out_ref.shape[1]
    out_ref[...] = tile_ref[:, pl.ds(pl.multiple_of(v_ref[0] * width, width), width), :]


def normal_taps(spreads_ref, view):
    spreads = spreads_ref[view, :, :TAPS]
    return spreads / jnp.sum(spreads, axis=1, keepdims=True)


def band(taps, offset):
    matrix = jnp.zeros(offset.shape, jnp.float32)
    for t in range(TAPS):
        matrix = jnp.where(offset == t, jnp.broadcast_to(taps[:, t : t + 1], offset.shape), matrix)
    return matrix


def bands(taps, adjoint):
    row = lax.broadcasted_iota(jnp.int32, (HALF, 9 * HALF), 0)
    lane = lax.broadcasted_iota(jnp.int32, (HALF, 9 * HALF), 1)
    first, last = lane < 3 * HALF, lane >= 6 * HALF
    column = jnp.where(first, lane, jnp.where(last, lane - 6 * HALF, lane - 3 * HALF))
    matrix = band(taps, column - row if adjoint else row - column + 2 * HALF)
    high = matrix.astype(jnp.bfloat16).astype(jnp.float32)
    return jnp.where(jnp.logical_or(first, last), high, matrix - high).astype(jnp.bfloat16)


def forward_bands_kernel(spreads_ref, x_ref, y_ref):
    for view in range(spreads_ref.shape[0]):
        normal = normal_taps(spreads_ref, view)
        x_ref[view] = bands(normal[0:1], False)
        y_ref[view * HALF : (view + 1) * HALF] = bands(normal[1:2], False)


def matrices_kernel(spreads_ref, x_ref, y_ref, forward_ref, adjoint_ref):
    row = lax.broadcasted_iota(jnp.int32, (LANES, LANES), 0)
    column = lax.broadcasted_iota(jnp.int32, (LANES, LANES), 1)
    for view in range(spreads_ref.shape[0]):
        normal = normal_taps(spreads_ref, view)
        x_ref[view] = bands(normal[0:1], True)
        y_ref[view] = bands(normal[1:2], True)
        for target, offset in ((forward_ref, column - row + HALF), (adjoint_ref, row - column + HALF)):
            high, low = split(band(normal[2:3], offset))
            for k in (0, LANES):
                target[view, k : k + LANES, :LANES] = high
                target[view, k : k + LANES, LANES:] = low


def banded(matrix, pieces):
    high, low = split(jnp.concatenate(pieces, axis=0))
    return jnp.dot(matrix, jnp.concatenate([high, high, low], axis=0), preferred_element_type=jnp.float32)


def beside(ref, count):
    return jnp.concatenate([ref[i] for i in range(count)], axis=1)


def blur_x(refs, matrix, out_ref):
    rows, width, _ = out_ref.shape
    flat = [ref.reshape(rows * width, LANES) for ref in refs]
    pieces = [jnp.concatenate([ref[pl.ds(j, rows, stride=width), :] for j in range(width)], axis=1) for ref in flat]
    blurred = banded(matrix, pieces)
    target = out_ref.reshape(rows * width, LANES)
    for j in range(width):
        target[pl.ds(j, rows, stride=width), :] = blurred[:, j * LANES : (j + 1) * LANES]


def blur_z(value, matrix):
    rows, width, _ = value.shape
    high, low = split(value.reshape(rows * width, LANES))
    product = jnp.dot(jnp.concatenate([high, low], axis=1), matrix, preferred_element_type=jnp.float32)
    return (product[:, :LANES] + product[:, LANES:]).reshape(rows, width, LANES)


def forward_y(refs, matrix_ref, out_ref):
    views, rows, width, _ = out_ref.shape
    blurred = banded(matrix_ref[...], [beside(ref, rows) for ref in refs])
    for view in range(views):
        for i in range(rows):
            out_ref[view, i] = blurred[view * width : (view + 1) * width, i * LANES : (i + 1) * LANES]


def forward_y_kernel(before_ref, own_ref, after_ref, matrix_ref, out_ref):
    forward_y((before_ref, own_ref, after_ref), matrix_ref, out_ref)


def first_forward_y_kernel(first, v_ref, tile_ref, across_ref, matrix_ref, out_ref, *part_refs):
    rows, width = out_ref.shape[1:3]
    views = tile_ref.shape[1] // width
    there = pl.ds(first, rows)
    for n, part_ref in enumerate(part_refs):
        place = v_ref[0] + n - 1
        inside = jnp.logical_and(place >= 0, place < views)

        @pl.when(inside)
        def _():
            part_ref[...] = tile_ref[there, pl.ds(pl.multiple_of(place * width, width), width), :]

        @pl.when(jnp.logical_not(inside))
        def _():
            part_ref[...] = across_ref[there]

    forward_y(part_refs, matrix_ref, out_ref)


def blurred_kernel(before_ref, own_ref, after_ref, bands_ref, matrix_ref, out_ref, mid_ref):
    for view in range(out_ref.shape[0]):
        blur_x([ref.at[view] for ref in (before_ref, own_ref, after_ref)], bands_ref[view], mid_ref.at[view])
        out_ref[view] = blur_z(mid_ref[view], matrix_ref[view])


def divide_kernel(first, data_ref, blurred_ref, out_ref):
    views, rows = out_ref.shape[:2]
    for view in range(views):
        out_ref[view] = data_ref[view, pl.ds(first, rows)] / blurred_ref[view]


def ratio_kernel(first, before_ref, own_ref, after_ref, bands_ref, matrix_ref, data_ref, out_ref, mid_ref):
    views, rows = out_ref.shape[:2]
    for view in range(views):
        blur_x([ref.at[view] for ref in (before_ref, own_ref, after_ref)], bands_ref[view], mid_ref.at[view])
        out_ref[view] = data_ref[view, pl.ds(first, rows)] / blur_z(mid_ref[view], matrix_ref[view])


def adjoint_x_kernel(before_ref, own_ref, after_ref, bands_ref, out_ref):
    for view in range(out_ref.shape[0]):
        blur_x([ref.at[view] for ref in (before_ref, own_ref, after_ref)], bands_ref[view], out_ref.at[view])


def update_kernel(first, before_ref, own_ref, after_ref, bands_ref, matrix_ref, estimate_ref, out_ref, mid_ref):
    views, rows = own_ref.shape[:2]
    total = None
    for view in range(views):
        blurred = banded(bands_ref[view], [beside(ref.at[view], rows) for ref in (before_ref, own_ref, after_ref)])
        for i in range(rows):
            mid_ref[view, i] = blurred[:, i * LANES : (i + 1) * LANES]
        terms = jnp.log(blur_z(mid_ref[view], matrix_ref[view]))
        total = terms if total is None else total + terms
    out_ref[...] = estimate_ref[pl.ds(first, rows)] * jnp.exp(total / views)


def collect_kernel(pieces_ref, out_ref):
    views, _, width, _ = pieces_ref.shape
    for view in range(views):
        out_ref[:, view * width : (view + 1) * width, :] = pieces_ref[view]


def shifted(size, by):
    return [(i, i + by) for i in range(size) if 0 <= i + by < size]


def onward(value, axes):
    return lax.ppermute(value, axes, shifted(lax.axis_size(axes), 1))


def back(value, axes):
    return lax.ppermute(value, axes, shifted(lax.axis_size(axes), -1))


def across(value):
    tiles, views = lax.axis_size("gy"), lax.axis_size("view")
    pairs = [(gy * views + views - 1, (gy + 1) * views) for gy in range(tiles - 1)]
    return lax.ppermute(value, ("gy", "view"), pairs + [(b, a) for a, b in pairs])


def exchanged(pieces):
    return lax.all_to_all(pieces, "view", 0, 0, tiled=True)


def body(estimate, views_data, spread_x, spread_y, spread_z):
    rows, width, depth = estimate.shape
    views = lax.axis_size("view")
    width = width // views
    half = rows // 2
    assert width == HALF and half == HALF and depth == LANES
    f32 = jnp.float32
    v = lax.axis_index("view")
    v_word = v.astype(jnp.int32).reshape(1)
    y = ("gy", "view")
    half_shape = ((views, half, width, depth), f32)
    bands_shape = ((views, HALF, 9 * HALF), jnp.bfloat16)
    matrix_shape = ((views, 2 * LANES, 2 * LANES), jnp.bfloat16)
    part = ((half, width, depth), f32)
    mid = [pltpu.VMEM(*half_shape)]

    own = call(part_kernel, [((rows, width, depth), f32)], [], v_word, estimate)[0]
    spreads = jnp.concatenate([spread_x, spread_y, spread_z, jnp.ones((5, TAPS), f32)])
    spreads = jnp.broadcast_to(jnp.pad(spreads, ((0, 0), (0, LANES - TAPS))), (views, 8, LANES))
    data = call(deal_kernel, [((views, rows, width, depth), f32)], [], views_data[0])[0]
    spreads = exchanged(spreads)
    data = exchanged(data)
    edge = across(own)
    forward_x, forward_y = call(
        forward_bands_kernel, [bands_shape, ((views * HALF, 9 * HALF), jnp.bfloat16)], [], spreads
    )
    adjoint_x, adjoint_y, forward_z, adjoint_z = call(
        matrices_kernel, [bands_shape, bands_shape, matrix_shape, matrix_shape], [], spreads
    )
    for step_number in range(ITERS):
        if step_number == 0:
            blurred = [
                call(
                    functools.partial(first_forward_y_kernel, n * half), [half_shape], [pltpu.VMEM(*part)] * 3,
                    v_word, estimate, edge, forward_y,
                )[0]
                for n in range(2)
            ]
        else:
            edges = [(onward(own[n], y), back(own[n], y)) for n in range(2)]
            blurred = [
                call(forward_y_kernel, [half_shape], [], edges[n][0], own[n], edges[n][1], forward_y)[0] for n in range(2)
            ]
        low, high = blurred
        before, after = onward(high, "gx"), back(low, "gx")
        ratios = []
        for first, rows_in in ((0, (before, low, high)), (half, (low, high, after))):
            if step_number == 0:
                blurred = call(blurred_kernel, [half_shape], mid, *rows_in, forward_x, forward_z)[0]
                ratios.append(call(functools.partial(divide_kernel, first), [half_shape], [], data, blurred)[0])
            else:
                kernel = functools.partial(ratio_kernel, first)
                ratios.append(call(kernel, [half_shape], mid, *rows_in, forward_x, forward_z, data)[0])
        ratio_low, ratio_high = ratios
        before, after = onward(ratio_high, "gx"), back(ratio_low, "gx")
        high = call(adjoint_x_kernel, [half_shape], [], ratio_low, ratio_high, after, adjoint_x)[0]
        low = call(adjoint_x_kernel, [half_shape], [], before, ratio_low, ratio_high, adjoint_x)[0]
        ins = [(onward(value, y), value, back(value, y), adjoint_y, adjoint_z) for value in (low, high)]
        olds = [(0, own[0]), (0, own[1])] if step_number else [(0, own), (half, own)]
        own = [
            call(functools.partial(update_kernel, first), [part], mid, *ins[n], old)[0]
            for n, (first, old) in enumerate(olds)
        ]
    share = rows // views
    pieces = exchanged(jnp.concatenate(own).reshape(views, share, width, depth))
    return call(collect_kernel, [((share, width * views, depth), f32)], [], pieces)[0]


def solution(mesh):
    in_specs = (
        P("gx", "gy", None),
        P("view", "gx", "gy", None),
        P("view", None),
        P("view", None),
        P("view", None),
    )
    out_specs = P(("gx", "view"), "gy", None)
    return jax.shard_map(body, mesh=mesh, in_specs=in_specs, out_specs=out_specs, check_vma=False)
```

```python
import functools

import jax
import jax.numpy as jnp
from jax import lax
from jax.experimental import pallas as pl
from jax.experimental.pallas import tpu as pltpu
from jax.sharding import PartitionSpec as P

ITERS = 2
TAPS = 33
HALF = 16
LANES = 128
VMEM = pl.BlockSpec(memory_space=pltpu.VMEM)
SMEM = pl.BlockSpec(memory_space=pltpu.SMEM)
ANY = pl.BlockSpec(memory_space=pl.ANY)


def call(kernel, outs, scratch, *args, away=(), mebibytes=10):
    specs = [SMEM if a.dtype == jnp.int32 else ANY if n in away else VMEM for n, a in enumerate(args)]
    return pl.pallas_call(
        kernel,
        out_shape=[jax.ShapeDtypeStruct(s, d) for s, d in outs],
        in_specs=specs,
        out_specs=[VMEM] * len(outs),
        scratch_shapes=scratch,
        compiler_params=pltpu.CompilerParams(vmem_limit_bytes=mebibytes * 2**20),
    )(*args)


def split(value):
    high = value.astype(jnp.bfloat16)
    low = (value - high.astype(jnp.float32)).astype(jnp.bfloat16)
    return high, low


def pack_kernel(data_ref, *refs):
    spreads_refs, (out_ref, tile_ref, taps_ref, arrived) = refs[:-4], refs[-4:]
    copies = [pltpu.make_async_copy(data_ref, tile_ref, arrived.at[0])]
    for n, spread_ref in enumerate(spreads_refs):
        copies.append(pltpu.make_async_copy(spread_ref, taps_ref.at[n], arrived.at[1 + n]))
    for copy in copies:
        copy.start()
    for copy in copies:
        copy.wait()
    views, length, _ = out_ref.shape
    rows, width = data_ref.shape[0], data_ref.shape[1] // views
    cells = rows * width
    for view in range(views):
        piece = tile_ref[:, view * width : (view + 1) * width, :].astype(jnp.float32)
        out_ref[view, :cells] = piece.reshape(cells, LANES)
        out_ref[view, cells:] = jnp.zeros((length - cells, LANES), jnp.float32)
        for n in range(len(spreads_refs)):
            out_ref[view, cells + n : cells + n + 1, :TAPS] = taps_ref[n]


def part_kernel(v_ref, tile_ref, out_ref):
    width = out_ref.shape[1]
    out_ref[...] = tile_ref[:, pl.ds(pl.multiple_of(v_ref[0] * width, width), width), :]


def shifted_taps(packed_ref, view, axis, rows, shift):
    row = packed_ref.shape[1] - 8 + axis
    spread = packed_ref[view, row : row + 1, :]
    taps = jnp.broadcast_to(spread / jnp.sum(spread, axis=1, keepdims=True), (rows, LANES))
    turned = pltpu.roll(taps, (LANES - shift) % LANES, 1, stride=1, stride_axis=0)
    a = lax.broadcasted_iota(jnp.int32, (rows, LANES), 0)
    b = lax.broadcasted_iota(jnp.int32, (rows, LANES), 1)
    t = b - a + shift
    return jnp.where(jnp.logical_and(t >= 0, t < TAPS), turned, 0.0)


def flipped(matrix):
    columns = matrix.T[:HALF]
    return jnp.concatenate([columns, jnp.zeros((HALF, LANES - columns.shape[1]), columns.dtype)], axis=1)


def store_bands(matrix, out_ref):
    width = 3 * HALF
    high = matrix.astype(jnp.bfloat16).astype(jnp.float32)
    lane = lax.broadcasted_iota(jnp.int32, (HALF, LANES), 1)
    again = pltpu.roll(high, 2 * width, 1)
    start = high + pltpu.roll(matrix - high, width, 1) + jnp.where(lane >= 2 * width, again, 0.0)
    out_ref[:, :LANES] = start.astype(jnp.bfloat16)
    out_ref[:, LANES:] = again[:, : 3 * width - LANES].astype(jnp.bfloat16)


def store_z(matrix, out_ref):
    high, low = split(matrix)
    for k in (0, LANES):
        out_ref[k : k + LANES, :LANES] = high
        out_ref[k : k + LANES, LANES:] = low


def forward_matrices_kernel(packed_ref, x_ref, y_ref, z_ref):
    for view in range(packed_ref.shape[0]):
        for axis, target in ((0, x_ref.at[view]), (1, y_ref.at[pl.ds(view * HALF, HALF)])):
            store_bands(flipped(shifted_taps(packed_ref, view, axis, 3 * HALF, 2 * HALF)), target)
        store_z(shifted_taps(packed_ref, view, 2, LANES, HALF), z_ref.at[view])


def adjoint_matrices_kernel(packed_ref, x_ref, y_ref, z_ref):
    for view in range(packed_ref.shape[0]):
        for axis, target in ((0, x_ref.at[view]), (1, y_ref.at[view])):
            store_bands(shifted_taps(packed_ref, view, axis, HALF, 0), target)
        store_z(shifted_taps(packed_ref, view, 2, LANES, HALF).T, z_ref.at[view])


def banded(matrix, pieces):
    high, low = split(jnp.concatenate(pieces, axis=0))
    return jnp.dot(matrix, jnp.concatenate([high, high, low], axis=0), preferred_element_type=jnp.float32)


def beside(ref, count):
    return jnp.concatenate([ref[i] for i in range(count)], axis=1)


def blur_x(refs, matrix, out_ref):
    rows, width, _ = out_ref.shape
    flat = [ref.reshape(rows * width, LANES) for ref in refs]
    pieces = [jnp.concatenate([ref[pl.ds(j, rows, stride=width), :] for j in range(width)], axis=1) for ref in flat]
    blurred = banded(matrix, pieces)
    target = out_ref.reshape(rows * width, LANES)
    for j in range(width):
        target[pl.ds(j, rows, stride=width), :] = blurred[:, j * LANES : (j + 1) * LANES]


def blur_z(value, matrix):
    rows, width, _ = value.shape
    high, low = split(value.reshape(rows * width, LANES))
    product = jnp.dot(jnp.concatenate([high, low], axis=1), matrix, preferred_element_type=jnp.float32)
    return (product[:, :LANES] + product[:, LANES:]).reshape(rows, width, LANES)


def forward_y(pieces, matrix_ref, out_ref):
    views, rows, width, _ = out_ref.shape
    blurred = banded(matrix_ref[...], pieces)
    for view in range(views):
        for i in range(rows):
            out_ref[view, i] = blurred[view * width : (view + 1) * width, i * LANES : (i + 1) * LANES]


def forward_y_kernel(before_ref, own_ref, after_ref, matrix_ref, out_ref):
    rows = own_ref.shape[0]
    forward_y([beside(ref, rows) for ref in (before_ref, own_ref, after_ref)], matrix_ref, out_ref)


def extended_kernel(v_ref, tile_ref, across_ref, *out_refs):
    rows, width = out_refs[0].shape[0], out_refs[0].shape[1] // 3
    views = tile_ref.shape[1] // width
    for n in range(3):
        place = v_ref[0] + n - 1
        inside = jnp.logical_and(place >= 0, place < views)
        for half, out_ref in enumerate(out_refs):
            there = pl.ds(half * rows, rows)

            @pl.when(inside)
            def _():
                columns = pl.ds(pl.multiple_of(place * width, width), width)
                out_ref[:, n * width : (n + 1) * width, :] = tile_ref[there, columns, :]

            @pl.when(jnp.logical_not(inside))
            def _():
                out_ref[:, n * width : (n + 1) * width, :] = across_ref[there]


def extended_y_kernel(*refs):
    count = len(refs) // 2
    matrix_ref = refs[count]
    for ext_ref, out_ref in zip(refs[:count], refs[count + 1 :]):
        forward_y([beside(ext_ref, ext_ref.shape[0])], matrix_ref, out_ref)


def ratio_kernel(first, before_ref, own_ref, after_ref, bands_ref, matrix_ref, data_ref, out_ref, mid_ref):
    views, rows, width, _ = out_ref.shape
    for view in range(views):
        blur_x([ref.at[view] for ref in (before_ref, own_ref, after_ref)], bands_ref[view], mid_ref.at[view])
        data = data_ref[view, pl.ds(first * width, rows * width)].reshape(rows, width, LANES)
        out_ref[view] = data / blur_z(mid_ref[view], matrix_ref[view])


def adjoint_x_kernel(before_ref, own_ref, after_ref, bands_ref, out_ref):
    for view in range(out_ref.shape[0]):
        blur_x([ref.at[view] for ref in (before_ref, own_ref, after_ref)], bands_ref[view], out_ref.at[view])


def update_kernel(first, before_ref, own_ref, after_ref, bands_ref, matrix_ref, estimate_ref, out_ref, mid_ref):
    views, rows = own_ref.shape[:2]
    total = None
    for view in range(views):
        blurred = banded(bands_ref[view], [beside(ref.at[view], rows) for ref in (before_ref, own_ref, after_ref)])
        for i in range(rows):
            mid_ref[view, i] = blurred[:, i * LANES : (i + 1) * LANES]
        terms = jnp.log(blur_z(mid_ref[view], matrix_ref[view]))
        total = terms if total is None else total + terms
    out_ref[...] = estimate_ref[pl.ds(first, rows)] * jnp.exp(total / views)


def collect_kernel(pieces_ref, out_ref):
    views, _, width, _ = pieces_ref.shape
    for view in range(views):
        out_ref[:, view * width : (view + 1) * width, :] = pieces_ref[view]


def shifted(size, by):
    return [(i, i + by) for i in range(size) if 0 <= i + by < size]


def onward(value, axes):
    return lax.ppermute(value, axes, shifted(lax.axis_size(axes), 1))


def back(value, axes):
    return lax.ppermute(value, axes, shifted(lax.axis_size(axes), -1))


def across(value):
    tiles, views = lax.axis_size("gy"), lax.axis_size("view")
    pairs = [(gy * views + views - 1, (gy + 1) * views) for gy in range(tiles - 1)]
    return lax.ppermute(value, ("gy", "view"), pairs + [(b, a) for a, b in pairs])


def exchanged(pieces):
    return lax.all_to_all(pieces, "view", 0, 0, tiled=True)


def body(estimate, views_data, spread_x, spread_y, spread_z):
    rows, width, depth = estimate.shape
    views = lax.axis_size("view")
    width = width // views
    half = rows // 2
    assert width == HALF and half == HALF and depth == LANES
    f32 = jnp.float32
    v = lax.axis_index("view")
    v_word = v.astype(jnp.int32).reshape(1)
    y = ("gy", "view")
    half_shape = ((views, half, width, depth), f32)
    bands_shape = ((views, HALF, 9 * HALF), jnp.bfloat16)
    matrix_shape = ((views, 2 * LANES, 2 * LANES), jnp.bfloat16)
    part = ((half, width, depth), f32)
    mid = [pltpu.VMEM(*half_shape)]

    own = call(part_kernel, [((rows, width, depth), f32)], [], v_word, estimate)[0]
    packed = call(
        pack_kernel, [((views, rows * width + 8, depth), f32)],
        [pltpu.VMEM(estimate.shape, views_data.dtype), pltpu.VMEM((3, 1, TAPS), f32), pltpu.SemaphoreType.DMA((4,))],
        views_data[0], spread_x, spread_y, spread_z, away=range(4), mebibytes=56,
    )[0]
    packed = exchanged(packed)
    ext_shape = ((half, 3 * width, depth), f32)
    low, high = call(extended_kernel, [ext_shape] * 2, [], v_word, estimate, across(own))
    rows_in = [onward(high, "gx"), low, high, back(low, "gx")]
    forward_x, forward_y, forward_z = call(
        forward_matrices_kernel, [bands_shape, ((views * HALF, 9 * HALF), jnp.bfloat16), matrix_shape], [], packed
    )
    adjoint_x, adjoint_y, adjoint_z = call(
        adjoint_matrices_kernel, [bands_shape, bands_shape, matrix_shape], [], packed
    )
    for step_number in range(ITERS):
        if step_number == 0:
            before, low, high, after = call(extended_y_kernel, [half_shape] * 4, [], *rows_in, forward_y)
        else:
            low, high = [
                call(forward_y_kernel, [half_shape], [], onward(value, y), value, back(value, y), forward_y)[0]
                for value in own
            ]
            before, after = onward(high, "gx"), back(low, "gx")
        ratio_low, ratio_high = [
            call(functools.partial(ratio_kernel, n * half), [half_shape], mid, *three, forward_x, forward_z, packed)[0]
            for n, three in enumerate(((before, low, high), (low, high, after)))
        ]
        before, after = onward(ratio_high, "gx"), back(ratio_low, "gx")
        high = call(adjoint_x_kernel, [half_shape], [], ratio_low, ratio_high, after, adjoint_x)[0]
        low = call(adjoint_x_kernel, [half_shape], [], before, ratio_low, ratio_high, adjoint_x)[0]
        ins = [(onward(value, y), value, back(value, y), adjoint_y, adjoint_z) for value in (low, high)]
        olds = [(0, own[0]), (0, own[1])] if step_number else [(0, own), (half, own)]
        own = [
            call(functools.partial(update_kernel, first), [part], mid, *ins[n], old)[0]
            for n, (first, old) in enumerate(olds)
        ]
    share = rows // views
    pieces = exchanged(jnp.concatenate(own).reshape(views, share, width, depth))
    return call(collect_kernel, [((share, width * views, depth), f32)], [], pieces)[0]


def solution(mesh):
    in_specs = (
        P("gx", "gy", None),
        P("view", "gx", "gy", None),
        P("view", None),
        P("view", None),
        P("view", None),
    )
    out_specs = P(("gx", "view"), "gy", None)
    return jax.shard_map(body, mesh=mesh, in_specs=in_specs, out_specs=out_specs, check_vma=False)
```

```python
import functools

import jax
import jax.numpy as jnp
from jax import lax
from jax.experimental import pallas as pl
from jax.experimental.pallas import tpu as pltpu
from jax.sharding import PartitionSpec as P

ITERS = 2
TAPS = 33
HALF = 16
LANES = 128
VMEM = pl.BlockSpec(memory_space=pltpu.VMEM)
SMEM = pl.BlockSpec(memory_space=pltpu.SMEM)
ANY = pl.BlockSpec(memory_space=pl.ANY)


def call(kernel, outs, scratch, *args, away=(), mebibytes=10):
    specs = [SMEM if a.dtype == jnp.int32 else ANY if n in away else VMEM for n, a in enumerate(args)]
    return pl.pallas_call(
        kernel,
        out_shape=[jax.ShapeDtypeStruct(s, d) for s, d in outs],
        in_specs=specs,
        out_specs=[VMEM] * len(outs),
        scratch_shapes=scratch,
        compiler_params=pltpu.CompilerParams(vmem_limit_bytes=mebibytes * 2**20),
    )(*args)


def split(value):
    high = value.astype(jnp.bfloat16)
    low = (value - high.astype(jnp.float32)).astype(jnp.bfloat16)
    return high, low


def pack_kernel(data_ref, *refs):
    spreads_refs, (out_ref, tile_ref, taps_ref, arrived) = refs[:-4], refs[-4:]
    copies = [pltpu.make_async_copy(data_ref, tile_ref, arrived.at[0])]
    for n, spread_ref in enumerate(spreads_refs):
        copies.append(pltpu.make_async_copy(spread_ref, taps_ref.at[n], arrived.at[1 + n]))
    for copy in copies:
        copy.start()
    for copy in copies:
        copy.wait()
    views, length, _ = out_ref.shape
    rows, width = data_ref.shape[0], data_ref.shape[1] // views
    cells = rows * width
    for view in range(views):
        piece = tile_ref[:, view * width : (view + 1) * width, :].astype(jnp.float32)
        out_ref[view, :cells] = piece.reshape(cells, LANES)
        out_ref[view, cells:] = jnp.zeros((length - cells, LANES), jnp.float32)
        for n in range(len(spreads_refs)):
            out_ref[view, cells + n : cells + n + 1, :TAPS] = taps_ref[n]


def part_kernel(v_ref, tile_ref, out_ref):
    width = out_ref.shape[1]
    out_ref[...] = tile_ref[:, pl.ds(pl.multiple_of(v_ref[0] * width, width), width), :]


def normal_taps(packed_ref):
    spreads = packed_ref[:, packed_ref.shape[1] - 8 :, :]
    sums = jnp.sum(spreads, axis=2, keepdims=True)
    return spreads / jnp.where(sums > 0.0, sums, 1.0)


def shifted_taps(taps, rows, shift):
    turned = pltpu.roll(jnp.broadcast_to(taps, (rows, LANES)), (LANES - shift) % LANES, 1, stride=1, stride_axis=0)
    a = lax.broadcasted_iota(jnp.int32, (rows, LANES), 0)
    b = lax.broadcasted_iota(jnp.int32, (rows, LANES), 1)
    t = b - a + shift
    return jnp.where(jnp.logical_and(t >= 0, t < TAPS), turned, 0.0)


def flipped(matrix):
    columns = matrix.T[:HALF]
    return jnp.concatenate([columns, jnp.zeros((HALF, LANES - columns.shape[1]), columns.dtype)], axis=1)


def store_bands(matrix, out_ref):
    width = 3 * HALF
    high = matrix.astype(jnp.bfloat16).astype(jnp.float32)
    lane = lax.broadcasted_iota(jnp.int32, (HALF, LANES), 1)
    again = pltpu.roll(high, 2 * width, 1)
    start = high + pltpu.roll(matrix - high, width, 1) + jnp.where(lane >= 2 * width, again, 0.0)
    out_ref[:, :LANES] = start.astype(jnp.bfloat16)
    out_ref[:, LANES:] = again[:, : 3 * width - LANES].astype(jnp.bfloat16)


def store_z(matrix, out_ref):
    high, low = split(matrix)
    for k in (0, LANES):
        out_ref[k : k + LANES, :LANES] = high
        out_ref[k : k + LANES, LANES:] = low


def forward_matrices_kernel(packed_ref, x_ref, y_ref, z_ref):
    normal = normal_taps(packed_ref)
    for view in range(packed_ref.shape[0]):
        for axis, target in ((0, x_ref.at[view]), (1, y_ref.at[pl.ds(view * HALF, HALF)])):
            store_bands(flipped(shifted_taps(normal[view, axis : axis + 1], 3 * HALF, 2 * HALF)), target)
        store_z(shifted_taps(normal[view, 2:3], LANES, HALF), z_ref.at[view])


def adjoint_matrices_kernel(packed_ref, x_ref, y_ref, z_ref):
    normal = normal_taps(packed_ref)
    for view in range(packed_ref.shape[0]):
        for axis, target in ((0, x_ref.at[view]), (1, y_ref.at[view])):
            store_bands(shifted_taps(normal[view, axis : axis + 1], HALF, 0), target)
        store_z(shifted_taps(normal[view, 2:3], LANES, HALF).T, z_ref.at[view])


def banded(matrix, pieces):
    high, low = split(jnp.concatenate(pieces, axis=0))
    return jnp.dot(matrix, jnp.concatenate([high, high, low], axis=0), preferred_element_type=jnp.float32)


def beside(ref, count):
    return jnp.concatenate([ref[i] for i in range(count)], axis=1)


def stacked(blurred):
    count = blurred.shape[1] // LANES
    return jnp.concatenate([blurred[:, j * LANES : (j + 1) * LANES] for j in range(count)], axis=0)


def blurred_x(refs, matrix):
    rows, width, _ = refs[0].shape
    flat = [ref.reshape(rows * width, LANES) for ref in refs]
    pieces = [jnp.concatenate([ref[pl.ds(j, rows, stride=width), :] for j in range(width)], axis=1) for ref in flat]
    return stacked(banded(matrix, pieces))


def by_rows(columns, out_ref):
    rows, width, _ = out_ref.shape
    target = out_ref.reshape(rows * width, LANES)
    for j in range(width):
        target[pl.ds(j, rows, stride=width), :] = columns[j * rows : (j + 1) * rows]


def blur_z(value, matrix):
    high, low = split(value)
    product = jnp.dot(jnp.concatenate([high, low], axis=1), matrix, preferred_element_type=jnp.float32)
    return product[:, :LANES] + product[:, LANES:]


def forward_y(pieces, matrix_ref, out_ref):
    views, rows, width, _ = out_ref.shape
    blurred = banded(matrix_ref[...], pieces)
    for view in range(views):
        for i in range(rows):
            out_ref[view, i] = blurred[view * width : (view + 1) * width, i * LANES : (i + 1) * LANES]


def forward_y_kernel(before_ref, own_ref, after_ref, matrix_ref, out_ref):
    rows = own_ref.shape[0]
    forward_y([beside(ref, rows) for ref in (before_ref, own_ref, after_ref)], matrix_ref, out_ref)


def extended_kernel(v_ref, tile_ref, across_ref, *out_refs):
    rows, width = out_refs[0].shape[0], out_refs[0].shape[1] // 3
    views = tile_ref.shape[1] // width
    for n in range(3):
        place = v_ref[0] + n - 1
        inside = jnp.logical_and(place >= 0, place < views)
        for half, out_ref in enumerate(out_refs):
            there = pl.ds(half * rows, rows)

            @pl.when(inside)
            def _():
                columns = pl.ds(pl.multiple_of(place * width, width), width)
                out_ref[:, n * width : (n + 1) * width, :] = tile_ref[there, columns, :]

            @pl.when(jnp.logical_not(inside))
            def _():
                out_ref[:, n * width : (n + 1) * width, :] = across_ref[there]


def extended_y_kernel(*refs):
    count = len(refs) // 2
    matrix_ref = refs[count]
    for ext_ref, out_ref in zip(refs[:count], refs[count + 1 :]):
        forward_y([beside(ext_ref, ext_ref.shape[0])], matrix_ref, out_ref)


def ratio_kernel(first, before_ref, own_ref, after_ref, bands_ref, matrix_ref, data_ref, out_ref):
    views, rows, width, _ = out_ref.shape
    for view in range(views):
        blurred = blurred_x([ref.at[view] for ref in (before_ref, own_ref, after_ref)], bands_ref[view])
        blurred = blur_z(blurred, matrix_ref[view])
        data = [data_ref[view, pl.ds(first * width + j, rows, stride=width), :] for j in range(width)]
        by_rows(jnp.concatenate(data, axis=0) / blurred, out_ref.at[view])


def adjoint_x_kernel(before_ref, own_ref, after_ref, bands_ref, out_ref):
    for view in range(out_ref.shape[0]):
        blurred = blurred_x([ref.at[view] for ref in (before_ref, own_ref, after_ref)], bands_ref[view])
        by_rows(blurred, out_ref.at[view])


def update_kernel(first, before_ref, own_ref, after_ref, bands_ref, matrix_ref, estimate_ref, out_ref):
    views, rows, width, _ = own_ref.shape
    total = None
    for view in range(views):
        blurred = banded(bands_ref[view], [beside(ref.at[view], rows) for ref in (before_ref, own_ref, after_ref)])
        terms = jnp.log(blur_z(stacked(blurred), matrix_ref[view]))
        total = terms if total is None else total + terms
    out_ref[...] = estimate_ref[pl.ds(first, rows)] * jnp.exp(total / views).reshape(rows, width, LANES)


def collect_kernel(pieces_ref, out_ref):
    views, _, width, _ = pieces_ref.shape
    for view in range(views):
        out_ref[:, view * width : (view + 1) * width, :] = pieces_ref[view]


def shifted(size, by):
    return [(i, i + by) for i in range(size) if 0 <= i + by < size]


def onward(value, axes):
    return lax.ppermute(value, axes, shifted(lax.axis_size(axes), 1))


def back(value, axes):
    return lax.ppermute(value, axes, shifted(lax.axis_size(axes), -1))


def across(value):
    tiles, views = lax.axis_size("gy"), lax.axis_size("view")
    pairs = [(gy * views + views - 1, (gy + 1) * views) for gy in range(tiles - 1)]
    return lax.ppermute(value, ("gy", "view"), pairs + [(b, a) for a, b in pairs])


def exchanged(pieces):
    return lax.all_to_all(pieces, "view", 0, 0, tiled=True)


def body(estimate, views_data, spread_x, spread_y, spread_z):
    rows, width, depth = estimate.shape
    views = lax.axis_size("view")
    width = width // views
    half = rows // 2
    assert width == HALF and half == HALF and depth == LANES
    f32 = jnp.float32
    v = lax.axis_index("view")
    v_word = v.astype(jnp.int32).reshape(1)
    y = ("gy", "view")
    half_shape = ((views, half, width, depth), f32)
    bands_shape = ((views, HALF, 9 * HALF), jnp.bfloat16)
    matrix_shape = ((views, 2 * LANES, 2 * LANES), jnp.bfloat16)
    part = ((half, width, depth), f32)

    own = call(part_kernel, [((rows, width, depth), f32)], [], v_word, estimate)[0]
    packed = call(
        pack_kernel, [((views, rows * width + 8, depth), f32)],
        [pltpu.VMEM(estimate.shape, views_data.dtype), pltpu.VMEM((3, 1, TAPS), f32), pltpu.SemaphoreType.DMA((4,))],
        views_data[0], spread_x, spread_y, spread_z, away=range(4), mebibytes=56,
    )[0]
    packed = exchanged(packed)
    ext_shape = ((half, 3 * width, depth), f32)
    low, high = call(extended_kernel, [ext_shape] * 2, [], v_word, estimate, across(own))
    rows_in = [onward(high, "gx"), low, high, back(low, "gx")]
    forward_x, forward_y, forward_z = call(
        forward_matrices_kernel, [bands_shape, ((views * HALF, 9 * HALF), jnp.bfloat16), matrix_shape], [], packed
    )
    adjoint_x, adjoint_y, adjoint_z = call(
        adjoint_matrices_kernel, [bands_shape, bands_shape, matrix_shape], [], packed
    )
    for step_number in range(ITERS):
        if step_number == 0:
            before, low, high, after = call(extended_y_kernel, [half_shape] * 4, [], *rows_in, forward_y)
        else:
            low, high = [
                call(forward_y_kernel, [half_shape], [], onward(value, y), value, back(value, y), forward_y)[0]
                for value in own
            ]
            before, after = onward(high, "gx"), back(low, "gx")
        ratio_low, ratio_high = [
            call(functools.partial(ratio_kernel, n * half), [half_shape], [], *three, forward_x, forward_z, packed)[0]
            for n, three in enumerate(((before, low, high), (low, high, after)))
        ]
        before, after = onward(ratio_high, "gx"), back(ratio_low, "gx")
        high = call(adjoint_x_kernel, [half_shape], [], ratio_low, ratio_high, after, adjoint_x)[0]
        low = call(adjoint_x_kernel, [half_shape], [], before, ratio_low, ratio_high, adjoint_x)[0]
        ins = [(onward(value, y), value, back(value, y), adjoint_y, adjoint_z) for value in (low, high)]
        olds = [(0, own[0]), (0, own[1])] if step_number else [(0, own), (half, own)]
        own = [
            call(functools.partial(update_kernel, first), [part], [], *ins[n], old)[0]
            for n, (first, old) in enumerate(olds)
        ]
    share = rows // views
    pieces = exchanged(jnp.concatenate(own).reshape(views, share, width, depth))
    return call(collect_kernel, [((share, width * views, depth), f32)], [], pieces)[0]


def solution(mesh):
    in_specs = (
        P("gx", "gy", None),
        P("view", "gx", "gy", None),
        P("view", None),
        P("view", None),
        P("view", None),
    )
    out_specs = P(("gx", "view"), "gy", None)
    return jax.shard_map(body, mesh=mesh, in_specs=in_specs, out_specs=out_specs, check_vma=False)
```

```python
import functools

import jax
import jax.numpy as jnp
from jax import lax
from jax.experimental import pallas as pl
from jax.experimental.pallas import tpu as pltpu
from jax.sharding import PartitionSpec as P

ITERS = 2
TAPS = 33
HALF = 16
LANES = 128
VMEM = pl.BlockSpec(memory_space=pltpu.VMEM)
SMEM = pl.BlockSpec(memory_space=pltpu.SMEM)
ANY = pl.BlockSpec(memory_space=pl.ANY)


def call(kernel, outs, scratch, *args, away=(), mebibytes=10):
    specs = [SMEM if a.dtype == jnp.int32 else ANY if n in away else VMEM for n, a in enumerate(args)]
    return pl.pallas_call(
        kernel,
        out_shape=[jax.ShapeDtypeStruct(s, d) for s, d in outs],
        in_specs=specs,
        out_specs=[VMEM] * len(outs),
        scratch_shapes=scratch,
        compiler_params=pltpu.CompilerParams(vmem_limit_bytes=mebibytes * 2**20),
    )(*args)


def split(value):
    high = value.astype(jnp.bfloat16)
    low = (value - high.astype(jnp.float32)).astype(jnp.bfloat16)
    return high, low


def pack_kernel(data_ref, *refs):
    spreads_refs, (out_ref, tile_ref, taps_ref, arrived) = refs[:-4], refs[-4:]
    copies = [pltpu.make_async_copy(data_ref, tile_ref, arrived.at[0])]
    for n, spread_ref in enumerate(spreads_refs):
        copies.append(pltpu.make_async_copy(spread_ref, taps_ref.at[n], arrived.at[1 + n]))
    for copy in copies:
        copy.start()
    for copy in copies:
        copy.wait()
    views, length, _ = out_ref.shape
    rows, width = data_ref.shape[0], data_ref.shape[1] // views
    cells = rows * width
    for view in range(views):
        piece = tile_ref[:, view * width : (view + 1) * width, :].astype(jnp.float32)
        out_ref[view, :cells] = piece.reshape(cells, LANES)
        out_ref[view, cells:] = jnp.zeros((length - cells, LANES), jnp.float32)
        for n in range(len(spreads_refs)):
            out_ref[view, cells + n : cells + n + 1, :TAPS] = taps_ref[n]


def part_kernel(v_ref, tile_ref, out_ref):
    width = out_ref.shape[1]
    out_ref[...] = tile_ref[:, pl.ds(pl.multiple_of(v_ref[0] * width, width), width), :]


def normal_taps(packed_ref):
    spreads = packed_ref[:, packed_ref.shape[1] - 8 :, :]
    sums = jnp.sum(spreads, axis=2, keepdims=True)
    return spreads / jnp.where(sums > 0.0, sums, 1.0)


def shifted_taps(taps, rows, shift):
    turned = pltpu.roll(jnp.broadcast_to(taps, (rows, LANES)), (LANES - shift) % LANES, 1, stride=1, stride_axis=0)
    a = lax.broadcasted_iota(jnp.int32, (rows, LANES), 0)
    b = lax.broadcasted_iota(jnp.int32, (rows, LANES), 1)
    t = b - a + shift
    return jnp.where(jnp.logical_and(t >= 0, t < TAPS), turned, 0.0)


def flipped(matrix):
    columns = matrix.T[:HALF]
    return jnp.concatenate([columns, jnp.zeros((HALF, LANES - columns.shape[1]), columns.dtype)], axis=1)


def store_bands(matrix, out_ref):
    width = 3 * HALF
    high = matrix.astype(jnp.bfloat16).astype(jnp.float32)
    lane = lax.broadcasted_iota(jnp.int32, (HALF, LANES), 1)
    again = pltpu.roll(high, 2 * width, 1)
    start = high + pltpu.roll(matrix - high, width, 1) + jnp.where(lane >= 2 * width, again, 0.0)
    out_ref[:, :LANES] = start.astype(jnp.bfloat16)
    out_ref[:, LANES:] = again[:, : 3 * width - LANES].astype(jnp.bfloat16)


def store_z(matrix, out_ref):
    high, low = split(matrix)
    out_ref[:, :LANES] = high
    out_ref[:, LANES:] = low


def forward_matrices_kernel(packed_ref, x_ref, y_ref, z_ref):
    normal = normal_taps(packed_ref)
    for view in range(packed_ref.shape[0]):
        for axis, target in ((0, x_ref.at[view]), (1, y_ref.at[pl.ds(view * HALF, HALF)])):
            store_bands(flipped(shifted_taps(normal[view, axis : axis + 1], 3 * HALF, 2 * HALF)), target)
        store_z(shifted_taps(normal[view, 2:3], LANES, HALF), z_ref.at[view])


def adjoint_matrices_kernel(packed_ref, x_ref, y_ref, z_ref):
    normal = normal_taps(packed_ref)
    for view in range(packed_ref.shape[0]):
        for axis, target in ((0, x_ref.at[view]), (1, y_ref.at[view])):
            store_bands(shifted_taps(normal[view, axis : axis + 1], HALF, 0), target)
        store_z(shifted_taps(normal[view, 2:3], LANES, HALF).T, z_ref.at[view])


def banded(matrix, pieces):
    high, low = split(jnp.concatenate(pieces, axis=0))
    return jnp.dot(matrix, jnp.concatenate([high, high, low], axis=0), preferred_element_type=jnp.float32)


def beside(ref, count):
    return jnp.concatenate([ref[i] for i in range(count)], axis=1)


def stacked(blurred):
    count = blurred.shape[1] // LANES
    return jnp.concatenate([blurred[:, j * LANES : (j + 1) * LANES] for j in range(count)], axis=0)


def blurred_x(refs, matrix):
    rows, width, _ = refs[0].shape
    flat = [ref.reshape(rows * width, LANES) for ref in refs]
    pieces = [jnp.concatenate([ref[pl.ds(j, rows, stride=width), :] for j in range(width)], axis=1) for ref in flat]
    return stacked(banded(matrix, pieces))


def by_rows(columns, out_ref):
    rows, width, _ = out_ref.shape
    target = out_ref.reshape(rows * width, LANES)
    for j in range(width):
        target[pl.ds(j, rows, stride=width), :] = columns[j * rows : (j + 1) * rows]


def blur_z(value, matrix):
    high, low = split(value)
    twice = jnp.concatenate([matrix, matrix], axis=0)
    product = jnp.dot(jnp.concatenate([high, low], axis=1), twice, preferred_element_type=jnp.float32)
    return product[:, :LANES] + product[:, LANES:]


def forward_y(pieces, matrix_ref, out_ref):
    views, rows, width, _ = out_ref.shape
    blurred = banded(matrix_ref[...], pieces)
    for view in range(views):
        for i in range(rows):
            out_ref[view, i] = blurred[view * width : (view + 1) * width, i * LANES : (i + 1) * LANES]


def forward_y_kernel(before_ref, own_ref, after_ref, matrix_ref, out_ref):
    rows = own_ref.shape[0]
    forward_y([beside(ref, rows) for ref in (before_ref, own_ref, after_ref)], matrix_ref, out_ref)


def extended_kernel(v_ref, tile_ref, across_ref, *out_refs):
    rows, width = out_refs[0].shape[0], out_refs[0].shape[1] // 3
    views = tile_ref.shape[1] // width
    for n in range(3):
        place = v_ref[0] + n - 1
        inside = jnp.logical_and(place >= 0, place < views)
        for half, out_ref in enumerate(out_refs):
            there = pl.ds(half * rows, rows)

            @pl.when(inside)
            def _():
                columns = pl.ds(pl.multiple_of(place * width, width), width)
                out_ref[:, n * width : (n + 1) * width, :] = tile_ref[there, columns, :]

            @pl.when(jnp.logical_not(inside))
            def _():
                out_ref[:, n * width : (n + 1) * width, :] = across_ref[there]


def extended_y_kernel(*refs):
    count = len(refs) // 2
    matrix_ref = refs[count]
    for ext_ref, out_ref in zip(refs[:count], refs[count + 1 :]):
        forward_y([beside(ext_ref, ext_ref.shape[0])], matrix_ref, out_ref)


def ratio_kernel(first, before_ref, own_ref, after_ref, bands_ref, matrix_ref, data_ref, out_ref):
    views, rows, width, _ = out_ref.shape
    for view in range(views):
        blurred = blurred_x([ref.at[view] for ref in (before_ref, own_ref, after_ref)], bands_ref[view])
        blurred = blur_z(blurred, matrix_ref[view])
        data = [data_ref[view, pl.ds(first * width + j, rows, stride=width), :] for j in range(width)]
        by_rows(jnp.concatenate(data, axis=0) / blurred, out_ref.at[view])


def adjoint_x_kernel(before_ref, own_ref, after_ref, bands_ref, out_ref):
    for view in range(out_ref.shape[0]):
        blurred = blurred_x([ref.at[view] for ref in (before_ref, own_ref, after_ref)], bands_ref[view])
        by_rows(blurred, out_ref.at[view])


def update_kernel(first, before_ref, own_ref, after_ref, bands_ref, matrix_ref, estimate_ref, out_ref):
    views, rows, width, _ = own_ref.shape
    total = None
    for view in range(views):
        blurred = banded(bands_ref[view], [beside(ref.at[view], rows) for ref in (before_ref, own_ref, after_ref)])
        terms = jnp.log(blur_z(stacked(blurred), matrix_ref[view]))
        total = terms if total is None else total + terms
    out_ref[...] = estimate_ref[pl.ds(first, rows)] * jnp.exp(total / views).reshape(rows, width, LANES)


def collect_kernel(pieces_ref, out_ref):
    views, _, width, _ = pieces_ref.shape
    for view in range(views):
        out_ref[:, view * width : (view + 1) * width, :] = pieces_ref[view]


def shifted(size, by):
    return [(i, i + by) for i in range(size) if 0 <= i + by < size]


def onward(value, axes):
    return lax.ppermute(value, axes, shifted(lax.axis_size(axes), 1))


def back(value, axes):
    return lax.ppermute(value, axes, shifted(lax.axis_size(axes), -1))


def across(value):
    tiles, views = lax.axis_size("gy"), lax.axis_size("view")
    pairs = [(gy * views + views - 1, (gy + 1) * views) for gy in range(tiles - 1)]
    return lax.ppermute(value, ("gy", "view"), pairs + [(b, a) for a, b in pairs])


def exchanged(pieces):
    return lax.all_to_all(pieces, "view", 0, 0, tiled=True)


def body(estimate, views_data, spread_x, spread_y, spread_z):
    rows, width, depth = estimate.shape
    views = lax.axis_size("view")
    width = width // views
    half = rows // 2
    assert width == HALF and half == HALF and depth == LANES
    f32 = jnp.float32
    v = lax.axis_index("view")
    v_word = v.astype(jnp.int32).reshape(1)
    y = ("gy", "view")
    half_shape = ((views, half, width, depth), f32)
    bands_shape = ((views, HALF, 9 * HALF), jnp.bfloat16)
    matrix_shape = ((views, LANES, 2 * LANES), jnp.bfloat16)
    part = ((half, width, depth), f32)

    own = call(part_kernel, [((rows, width, depth), f32)], [], v_word, estimate)[0]
    packed = call(
        pack_kernel, [((views, rows * width + 8, depth), f32)],
        [pltpu.VMEM(estimate.shape, views_data.dtype), pltpu.VMEM((3, 1, TAPS), f32), pltpu.SemaphoreType.DMA((4,))],
        views_data[0], spread_x, spread_y, spread_z, away=range(4), mebibytes=56,
    )[0]
    packed = exchanged(packed)
    ext_shape = ((half, 3 * width, depth), f32)
    low, high = call(extended_kernel, [ext_shape] * 2, [], v_word, estimate, across(own))
    rows_in = [onward(high, "gx"), low, high, back(low, "gx")]
    forward_x, forward_y, forward_z = call(
        forward_matrices_kernel, [bands_shape, ((views * HALF, 9 * HALF), jnp.bfloat16), matrix_shape], [], packed
    )
    adjoint_x, adjoint_y, adjoint_z = call(
        adjoint_matrices_kernel, [bands_shape, bands_shape, matrix_shape], [], packed
    )
    for step_number in range(ITERS):
        if step_number == 0:
            before, low, high, after = call(extended_y_kernel, [half_shape] * 4, [], *rows_in, forward_y)
        else:
            low, high = [
                call(forward_y_kernel, [half_shape], [], onward(value, y), value, back(value, y), forward_y)[0]
                for value in own
            ]
            before, after = onward(high, "gx"), back(low, "gx")
        ratio_low, ratio_high = [
            call(functools.partial(ratio_kernel, n * half), [half_shape], [], *three, forward_x, forward_z, packed)[0]
            for n, three in enumerate(((before, low, high), (low, high, after)))
        ]
        before, after = onward(ratio_high, "gx"), back(ratio_low, "gx")
        high = call(adjoint_x_kernel, [half_shape], [], ratio_low, ratio_high, after, adjoint_x)[0]
        low = call(adjoint_x_kernel, [half_shape], [], before, ratio_low, ratio_high, adjoint_x)[0]
        ins = [(onward(value, y), value, back(value, y), adjoint_y, adjoint_z) for value in (low, high)]
        olds = [(0, own[0]), (0, own[1])] if step_number else [(0, own), (half, own)]
        own = [
            call(functools.partial(update_kernel, first), [part], [], *ins[n], old)[0]
            for n, (first, old) in enumerate(olds)
        ]
    share = rows // views
    pieces = exchanged(jnp.concatenate(own).reshape(views, share, width, depth))
    return call(collect_kernel, [((share, width * views, depth), f32)], [], pieces)[0]


def solution(mesh):
    in_specs = (
        P("gx", "gy", None),
        P("view", "gx", "gy", None),
        P("view", None),
        P("view", None),
        P("view", None),
    )
    out_specs = P(("gx", "view"), "gy", None)
    return jax.shard_map(body, mesh=mesh, in_specs=in_specs, out_specs=out_specs, check_vma=False)
```

```python
import functools

import jax
import jax.numpy as jnp
from jax import lax
from jax.experimental import pallas as pl
from jax.experimental.pallas import tpu as pltpu
from jax.sharding import PartitionSpec as P

ITERS = 2
TAPS = 33
HALF = 16
LANES = 128
VMEM = pl.BlockSpec(memory_space=pltpu.VMEM)
SMEM = pl.BlockSpec(memory_space=pltpu.SMEM)
ANY = pl.BlockSpec(memory_space=pl.ANY)


def call(kernel, outs, scratch, *args, away=(), mebibytes=10):
    specs = [SMEM if a.dtype == jnp.int32 else ANY if n in away else VMEM for n, a in enumerate(args)]
    return pl.pallas_call(
        kernel,
        out_shape=[jax.ShapeDtypeStruct(s, d) for s, d in outs],
        in_specs=specs,
        out_specs=[VMEM] * len(outs),
        scratch_shapes=scratch,
        compiler_params=pltpu.CompilerParams(vmem_limit_bytes=mebibytes * 2**20),
    )(*args)


def split(value):
    high = value.astype(jnp.bfloat16)
    low = (value - high.astype(jnp.float32)).astype(jnp.bfloat16)
    return high, low


def pack_kernel(data_ref, *refs):
    spreads_refs, (out_ref, tile_ref, taps_ref, arrived) = refs[:-4], refs[-4:]
    copies = [pltpu.make_async_copy(data_ref, tile_ref, arrived.at[0])]
    for n, spread_ref in enumerate(spreads_refs):
        copies.append(pltpu.make_async_copy(spread_ref, taps_ref.at[n], arrived.at[1 + n]))
    for copy in copies:
        copy.start()
    for copy in copies:
        copy.wait()
    views, length, _ = out_ref.shape
    rows, width = data_ref.shape[0], data_ref.shape[1] // views
    cells = rows * width
    for view in range(views):
        piece = tile_ref[:, view * width : (view + 1) * width, :].astype(jnp.float32)
        out_ref[view, :cells] = piece.reshape(cells, LANES)
        out_ref[view, cells:] = jnp.zeros((length - cells, LANES), jnp.float32)
        for n in range(len(spreads_refs)):
            out_ref[view, cells + n : cells + n + 1, :TAPS] = taps_ref[n]


def part_kernel(v_ref, tile_ref, out_ref):
    width = out_ref.shape[1]
    out_ref[...] = tile_ref[:, pl.ds(pl.multiple_of(v_ref[0] * width, width), width), :]


def normal_taps(packed_ref):
    spreads = packed_ref[:, packed_ref.shape[1] - 8 :, :]
    sums = jnp.sum(spreads, axis=2, keepdims=True)
    return spreads / jnp.where(sums > 0.0, sums, 1.0)


def shifted_taps(taps, rows, shift):
    turned = pltpu.roll(jnp.broadcast_to(taps, (rows, LANES)), (LANES - shift) % LANES, 1, stride=1, stride_axis=0)
    a = lax.broadcasted_iota(jnp.int32, (rows, LANES), 0)
    b = lax.broadcasted_iota(jnp.int32, (rows, LANES), 1)
    t = b - a + shift
    return jnp.where(jnp.logical_and(t >= 0, t < TAPS), turned, 0.0)


def flipped(matrix):
    columns = matrix.T[:HALF]
    return jnp.concatenate([columns, jnp.zeros((HALF, LANES - columns.shape[1]), columns.dtype)], axis=1)


def store_bands(matrix, out_ref):
    width = 3 * HALF
    high = matrix.astype(jnp.bfloat16).astype(jnp.float32)
    lane = lax.broadcasted_iota(jnp.int32, (HALF, LANES), 1)
    again = pltpu.roll(high, 2 * width, 1)
    start = high + pltpu.roll(matrix - high, width, 1) + jnp.where(lane >= 2 * width, again, 0.0)
    out_ref[:, :LANES] = start.astype(jnp.bfloat16)
    out_ref[:, LANES:] = again[:, : 3 * width - LANES].astype(jnp.bfloat16)


def store_z(matrix, out_ref):
    high, low = split(matrix)
    out_ref[:, :LANES] = high
    out_ref[:, LANES:] = low


def forward_matrices_kernel(packed_ref, x_ref, y_ref, z_ref):
    normal = normal_taps(packed_ref)
    for view in range(packed_ref.shape[0]):
        for axis, target in ((0, x_ref.at[view]), (1, y_ref.at[pl.ds(view * HALF, HALF)])):
            store_bands(flipped(shifted_taps(normal[view, axis : axis + 1], 3 * HALF, 2 * HALF)), target)
        store_z(shifted_taps(normal[view, 2:3], LANES, HALF), z_ref.at[view])


def adjoint_matrices_kernel(packed_ref, x_ref, y_ref, z_ref):
    normal = normal_taps(packed_ref)
    for view in range(packed_ref.shape[0]):
        for axis, target in ((0, x_ref.at[view]), (1, y_ref.at[view])):
            store_bands(shifted_taps(normal[view, axis : axis + 1], HALF, 0), target)
        store_z(shifted_taps(normal[view, 2:3], LANES, HALF).T, z_ref.at[view])


def banded(matrix, pieces):
    high, low = split(jnp.concatenate(pieces, axis=0))
    return jnp.dot(matrix, jnp.concatenate([high, high, low], axis=0), preferred_element_type=jnp.float32)


def beside(ref, count):
    return jnp.concatenate([ref[i] for i in range(count)], axis=1)


def stacked(blurred):
    count = blurred.shape[1] // LANES
    return jnp.concatenate([blurred[:, j * LANES : (j + 1) * LANES] for j in range(count)], axis=0)


def blurred_x(refs, matrix):
    rows, width, _ = refs[0].shape
    flat = [ref.reshape(rows * width, LANES) for ref in refs]
    pieces = [jnp.concatenate([ref[pl.ds(j, rows, stride=width), :] for j in range(width)], axis=1) for ref in flat]
    return stacked(banded(matrix, pieces))


def by_rows(columns, out_ref):
    rows, width, _ = out_ref.shape
    target = out_ref.reshape(rows * width, LANES)
    for j in range(width):
        target[pl.ds(j, rows, stride=width), :] = columns[j * rows : (j + 1) * rows]


def blur_z(value, matrix):
    high, low = split(value)
    twice = jnp.concatenate([matrix, matrix], axis=0)
    product = jnp.dot(jnp.concatenate([high, low], axis=1), twice, preferred_element_type=jnp.float32)
    return product[:, :LANES] + product[:, LANES:]


def forward_y(pieces, matrix_ref, out_ref):
    views, rows, width, _ = out_ref.shape
    blurred = banded(matrix_ref[...], pieces)
    for view in range(views):
        for i in range(rows):
            out_ref[view, i] = blurred[view * width : (view + 1) * width, i * LANES : (i + 1) * LANES]


def forward_y_kernel(before_ref, own_ref, after_ref, matrix_ref, out_ref):
    rows = own_ref.shape[0]
    forward_y([beside(ref, rows) for ref in (before_ref, own_ref, after_ref)], matrix_ref, out_ref)


def extended_kernel(v_ref, tile_ref, across_ref, *out_refs):
    rows, width = out_refs[0].shape[0], out_refs[0].shape[1] // 3
    views = tile_ref.shape[1] // width
    for n in range(3):
        place = v_ref[0] + n - 1
        inside = jnp.logical_and(place >= 0, place < views)
        for half, out_ref in enumerate(out_refs):
            there = pl.ds(half * rows, rows)

            @pl.when(inside)
            def _():
                columns = pl.ds(pl.multiple_of(place * width, width), width)
                out_ref[:, n * width : (n + 1) * width, :] = tile_ref[there, columns, :]

            @pl.when(jnp.logical_not(inside))
            def _():
                out_ref[:, n * width : (n + 1) * width, :] = across_ref[there]


def extended_y_kernel(*refs):
    count = len(refs) // 2
    matrix_ref = refs[count]
    for ext_ref, out_ref in zip(refs[:count], refs[count + 1 :]):
        forward_y([beside(ext_ref, ext_ref.shape[0])], matrix_ref, out_ref)


def ratio_kernel(first, before_ref, own_ref, after_ref, bands_ref, matrix_ref, data_ref, out_ref):
    views, rows, width, _ = out_ref.shape
    for view in range(views):
        blurred = blurred_x([ref.at[view] for ref in (before_ref, own_ref, after_ref)], bands_ref[view])
        blurred = blur_z(blurred, matrix_ref[view])
        data = [data_ref[view, pl.ds(first * width + j, rows, stride=width), :] for j in range(width)]
        by_rows(jnp.concatenate(data, axis=0) / blurred, out_ref.at[view])


def adjoint_x_kernel(before_ref, own_ref, after_ref, bands_ref, out_ref):
    for view in range(out_ref.shape[0]):
        blurred = blurred_x([ref.at[view] for ref in (before_ref, own_ref, after_ref)], bands_ref[view])
        by_rows(blurred, out_ref.at[view])


def update_kernel(first, before_ref, own_ref, after_ref, bands_ref, matrix_ref, estimate_ref, out_ref):
    views, rows, width, _ = own_ref.shape
    backs = []
    for view in range(views):
        blurred = banded(bands_ref[view], [beside(ref.at[view], rows) for ref in (before_ref, own_ref, after_ref)])
        backs.append(blur_z(stacked(blurred), matrix_ref[view]))
    total = sum(jnp.log(backs[n] * backs[n + 1]) for n in range(0, views, 2))
    out_ref[...] = estimate_ref[pl.ds(first, rows)] * jnp.exp(total / views).reshape(rows, width, LANES)


def collect_kernel(pieces_ref, out_ref):
    views, _, width, _ = pieces_ref.shape
    for view in range(views):
        out_ref[:, view * width : (view + 1) * width, :] = pieces_ref[view]


def shifted(size, by):
    return [(i, i + by) for i in range(size) if 0 <= i + by < size]


def onward(value, axes):
    return lax.ppermute(value, axes, shifted(lax.axis_size(axes), 1))


def back(value, axes):
    return lax.ppermute(value, axes, shifted(lax.axis_size(axes), -1))


def across(value):
    tiles, views = lax.axis_size("gy"), lax.axis_size("view")
    pairs = [(gy * views + views - 1, (gy + 1) * views) for gy in range(tiles - 1)]
    return lax.ppermute(value, ("gy", "view"), pairs + [(b, a) for a, b in pairs])


def exchanged(pieces):
    return lax.all_to_all(pieces, "view", 0, 0, tiled=True)


def body(estimate, views_data, spread_x, spread_y, spread_z):
    rows, width, depth = estimate.shape
    views = lax.axis_size("view")
    width = width // views
    half = rows // 2
    assert width == HALF and half == HALF and depth == LANES
    f32 = jnp.float32
    v = lax.axis_index("view")
    v_word = v.astype(jnp.int32).reshape(1)
    y = ("gy", "view")
    half_shape = ((views, half, width, depth), f32)
    bands_shape = ((views, HALF, 9 * HALF), jnp.bfloat16)
    matrix_shape = ((views, LANES, 2 * LANES), jnp.bfloat16)
    part = ((half, width, depth), f32)

    own = call(part_kernel, [((rows, width, depth), f32)], [], v_word, estimate)[0]
    packed = call(
        pack_kernel, [((views, rows * width + 8, depth), f32)],
        [pltpu.VMEM(estimate.shape, views_data.dtype), pltpu.VMEM((3, 1, TAPS), f32), pltpu.SemaphoreType.DMA((4,))],
        views_data[0], spread_x, spread_y, spread_z, away=range(4), mebibytes=56,
    )[0]
    packed = exchanged(packed)
    ext_shape = ((half, 3 * width, depth), f32)
    low, high = call(extended_kernel, [ext_shape] * 2, [], v_word, estimate, across(own))
    rows_in = [onward(high, "gx"), low, high, back(low, "gx")]
    forward_x, forward_y, forward_z = call(
        forward_matrices_kernel, [bands_shape, ((views * HALF, 9 * HALF), jnp.bfloat16), matrix_shape], [], packed
    )
    adjoint_x, adjoint_y, adjoint_z = call(
        adjoint_matrices_kernel, [bands_shape, bands_shape, matrix_shape], [], packed
    )
    for step_number in range(ITERS):
        if step_number == 0:
            before, low, high, after = call(extended_y_kernel, [half_shape] * 4, [], *rows_in, forward_y)
        else:
            low, high = [
                call(forward_y_kernel, [half_shape], [], onward(value, y), value, back(value, y), forward_y)[0]
                for value in own
            ]
            before, after = onward(high, "gx"), back(low, "gx")
        ratio_low, ratio_high = [
            call(functools.partial(ratio_kernel, n * half), [half_shape], [], *three, forward_x, forward_z, packed)[0]
            for n, three in enumerate(((before, low, high), (low, high, after)))
        ]
        before, after = onward(ratio_high, "gx"), back(ratio_low, "gx")
        high = call(adjoint_x_kernel, [half_shape], [], ratio_low, ratio_high, after, adjoint_x)[0]
        low = call(adjoint_x_kernel, [half_shape], [], before, ratio_low, ratio_high, adjoint_x)[0]
        ins = [(onward(value, y), value, back(value, y), adjoint_y, adjoint_z) for value in (low, high)]
        olds = [(0, own[0]), (0, own[1])] if step_number else [(0, own), (half, own)]
        own = [
            call(functools.partial(update_kernel, first), [part], [], *ins[n], old)[0]
            for n, (first, old) in enumerate(olds)
        ]
    share = rows // views
    pieces = exchanged(jnp.concatenate(own).reshape(views, share, width, depth))
    return call(collect_kernel, [((share, width * views, depth), f32)], [], pieces)[0]


def solution(mesh):
    in_specs = (
        P("gx", "gy", None),
        P("view", "gx", "gy", None),
        P("view", None),
        P("view", None),
        P("view", None),
    )
    out_specs = P(("gx", "view"), "gy", None)
    return jax.shard_map(body, mesh=mesh, in_specs=in_specs, out_specs=out_specs, check_vma=False)
```
